256 devices in a mesh: batch: 2 (over core), gz: 8 (over z), gy: 16 (over x, y).
Axes of the slice: x: 4, y: 4, z: 8, core: 2. Of those that a mesh axis runs over, the one named last changes fastest.
Arguments:
- volume: float32 [2, 4, 64, 256, 512], P('batch', None, 'gz', 'gy'), may hold values from -20 to 20
- conv_one: bfloat16 [16, 4, 3, 3, 3], replicated, may hold values from -0.625 to 0.625
- conv_two: bfloat16 [32, 16, 3, 3, 3], replicated, may hold values from -0.3125 to 0.3125
- conv_three: bfloat16 [64, 32, 3, 3, 3], replicated, may hold values from -0.21875 to 0.21875
- head_weight: float32 [4, 64], replicated, may hold values from -3 to 3
- targets: float32 [2, 4], P('batch'), may hold values from -4 to 4
Outputs:
- update_one: float32 [16, 4, 3, 3, 3], replicated
- update_two: float32 [32, 16, 3, 3, 3], replicated
- update_three: float32 [64, 32, 3, 3, 3], replicated
- update_head: float32 [4, 64], replicated
- total_loss: float32 [], replicated
The draws below stay inside these ranges and needn't reach their ends.
All inputs are finite; a program needn't handle non-finite values.
Results may differ from the reference program's by a relative error of at most 0.012.
Values may be sent and summed in bfloat16 or wider, within the bound.
No kernel may reach another device: no remote copies, remote signals or barrier semaphores. Data moves between devices by JAX's collectives and lax.ppermute only.
A program may use at most 192 MiB of HBM per device.

```python
import math
import jax
import jax.numpy as jnp
from jax import lax

CIN = 4
C1 = 16
C2 = 32
C3 = 64
OUTS = 4
NX = 512
VOLUMES = 2
NZ = 64
NY = 256


def draw_volume(key, part):
    key = jax.random.fold_in(key, 7)
    depth_pos = jnp.arange(NZ, dtype=jnp.float32) / NZ
    height_pos = jnp.arange(NY, dtype=jnp.float32) / NY
    random_part = jnp.clip(jax.random.normal(key, (VOLUMES, CIN, NZ, NY, NX), jnp.float32), -6.0, 6.0)
    growth = math.log(3.0)
    ramp_scale = jnp.exp(growth * (depth_pos[:, None] + height_pos[None, :] - 1.0))
    return random_part * ramp_scale[None, None, :, :, None]


def block_scale(own_key, dims, cuts, low, top_value):
    def one(axis_at, blocks):
        steps = jax.random.uniform(jax.random.fold_in(jax.random.fold_in(own_key, 6), axis_at), (blocks,), jnp.float32, low / len(cuts), top_value / len(cuts))
        return jnp.repeat(jnp.exp(steps), dims[axis_at] // blocks).reshape((-1,) + (1,) * (len(dims) - axis_at - 1))

    loudness = one(*cuts[0])
    for cut in cuts[1:]:
        loudness = loudness * one(*cut)
    return loudness


def gaussian(rng, dims, spread, limit, cuts=(), held_as=jnp.bfloat16):
    values = jax.random.normal(rng, dims, jnp.float32) * spread
    if len(cuts) > 0:
        values = block_scale(rng, dims, cuts, -0.22, 0.18) * values
    return jnp.clip(values, min=-limit, max=limit).astype(held_as)


def setup_inputs(seed: int = 0) -> dict:
    key_of = jax.random.split(jax.random.key(seed), 7)
    return {
        "volume": draw_volume(jax.random.fold_in(key_of[6], 71), 0),
        "conv_one": gaussian(key_of[1], (C1, CIN, 3, 3, 3), (27 * CIN) ** -0.5, 0.625),
        "conv_two": gaussian(key_of[2], (C2, C1, 3, 3, 3), (27 * C1) ** -0.5, 0.3125),
        "conv_three": gaussian(key_of[3], (C3, C2, 3, 3, 3), (27 * C2) ** -0.5, 0.21875),
        "head_weight": gaussian(key_of[4], (OUTS, C3), 0.5, 3.0, (), jnp.float32),
        "targets": gaussian(key_of[5], (VOLUMES, OUTS), 1.0, 4.0, ((0, 2),), jnp.float32),
    }


epsilon = 1e-06
highest = lax.Precision.HIGHEST

def convolve(source, kernel):
    return lax.conv_general_dilated(source.astype(jnp.float32), kernel.astype(jnp.float32), (2, 2, 2), [(1, 1), (1, 1), (1, 1)], dimension_numbers=('NCDHW', 'OIDHW', 'NCDHW'), precision=highest)

def activate(pre_act):
    return 0.65 * pre_act + 0.35 * (jnp.sqrt(pre_act * pre_act + 1.0) - 1.0)

def slope_of(pre_act):
    return 0.65 + 0.35 * pre_act / jnp.sqrt(pre_act * pre_act + 1.0)

def normalized(gradient):
    return gradient / jnp.sqrt(jnp.mean(gradient * gradient) + epsilon)

def weight_grad(source, errors, kernel):
    source_f = source.astype(jnp.float32)
    _, pullback = jax.vjp(lambda weights: convolve(source_f, weights), kernel.astype(jnp.float32))
    return pullback(errors.astype(jnp.float32))[0]

def input_grad(source, errors, kernel):
    kernel_f = kernel.astype(jnp.float32)
    _, pullback = jax.vjp(lambda values: convolve(values, kernel_f), source.astype(jnp.float32))
    return pullback(errors.astype(jnp.float32))[0]

def reference(volume, conv_one, conv_two, conv_three, head_weight, targets):
    inputs = volume.astype(jnp.bfloat16)
    pre_one = convolve(inputs, conv_one)
    act_one = activate(pre_one).astype(jnp.bfloat16)
    pre_two = convolve(act_one, conv_two)
    act_two = activate(pre_two).astype(jnp.bfloat16)
    pre_three = convolve(act_two, conv_three)
    act_three = activate(pre_three).astype(jnp.bfloat16)
    cell_count = pre_three.shape[2] * pre_three.shape[3] * pre_three.shape[4]
    pooled = lax.optimization_barrier(jnp.sum(act_three.astype(jnp.float32), axis=(2, 3, 4))) / cell_count
    predicted = jnp.dot(pooled, head_weight.T, precision=highest)
    errors = predicted - targets
    total_loss = 0.5 * jnp.sum(errors * errors)
    grad_head = jnp.dot(errors.T, pooled, precision=highest)
    back_pool = jnp.dot(errors, head_weight, precision=highest) / cell_count
    err_three = (back_pool[:, :, None, None, None] * slope_of(pre_three)).astype(jnp.bfloat16)
    grad_three = weight_grad(act_two, err_three, conv_three)
    back_two = input_grad(act_two, err_three, conv_three)
    err_two = (back_two * slope_of(pre_two)).astype(jnp.bfloat16)
    grad_two = weight_grad(act_one, err_two, conv_two)
    back_one = input_grad(act_one, err_two, conv_two)
    err_one = (back_one * slope_of(pre_one)).astype(jnp.bfloat16)
    grad_one = weight_grad(inputs, err_one, conv_one)
    return (normalized(grad_one), normalized(grad_two), normalized(grad_three), normalized(grad_head), total_loss)
```

```python
import jax
import jax.numpy as jnp
from jax import lax
from jax.sharding import PartitionSpec as P

epsilon = 1e-06
highest = lax.Precision.HIGHEST
layout = ("NCDHW", "OIDHW", "NCDHW")


def passed_along(x, axis, by):
    count = lax.axis_size(axis)
    pairs = [(i, i + by) for i in range(count) if 0 <= i + by < count]
    return lax.ppermute(x, axis, pairs)


def as_sent(x):
    return jax.tree.map(lambda a: a.astype(jnp.bfloat16) if a.dtype == jnp.float32 else a, x)


def activate(pre_act):
    return 0.65 * pre_act + 0.35 * (jnp.sqrt(pre_act * pre_act + 1.0) - 1.0)


def slope_of(pre_act):
    return 0.65 + 0.35 * pre_act / jnp.sqrt(pre_act * pre_act + 1.0)


def normalized(gradient):
    return gradient / jnp.sqrt(jnp.mean(gradient * gradient) + epsilon)


def gathered(x, axes):
    count = lax.axis_size(axes)
    return lax.all_to_all(jnp.broadcast_to(x[None], (count,) + x.shape), axes, 0, 0)


def summed_over_volume(x):
    return jnp.sum(gathered(x, ("gz", "gy")), axis=0)


def summed_over_all(terms):
    sizes = [t.size for t in terms]
    total = sum(sizes)
    columns = lax.axis_size("gy")
    width = -(-total // (columns * 1024)) * 8
    flat = jnp.concatenate([t.reshape(-1) for t in terms])
    flat = jnp.pad(flat, (0, columns * width * 128 - total)).reshape(columns, width, 128)
    own = jnp.sum(lax.all_to_all(flat, "gy", 0, 0), axis=0)
    own = jnp.sum(gathered(own, ("batch", "gz")), axis=0)
    flat = gathered(own, "gy").reshape(-1)
    out, at = [], 0
    for term, size in zip(terms, sizes):
        out.append(flat[at : at + size].reshape(term.shape))
        at += size
    return out


def extend(source):
    got_row = passed_along(source[:, :, -1:, :], "gy", 1)
    widened = jnp.concatenate([got_row, source], axis=2)
    lower = passed_along(widened[:, -1:, :, :], "gz", 1)
    extended = jnp.concatenate([lower, widened], axis=1)
    return jnp.pad(extended, ((0, 0), (0, 0), (0, 0), (1, 0)))


def local_conv(extended, kernel):
    return lax.conv_general_dilated(
        extended[None],
        kernel,
        (2, 2, 2),
        [(0, 0), (0, 0), (0, 0)],
        dimension_numbers=layout,
        preferred_element_type=jnp.float32,
    )[0]


def exact_conv(extended, kernel):
    return lax.conv_general_dilated(
        extended[None],
        kernel,
        (2, 2, 2),
        [(0, 0), (0, 0), (0, 0)],
        dimension_numbers=layout,
        precision=highest,
    )[0]


def forward_layer(source, kernel):
    extended = extend(source)
    return (extended, local_conv(extended, kernel))


def return_rims(grid):
    got_plane = passed_along(grid[:, 0:1, :, :].astype(jnp.bfloat16), "gz", -1).astype(jnp.float32)
    remain = grid[:, 1:, :, :]
    remain = remain + jnp.pad(got_plane, ((0, 0), (remain.shape[1] - 1, 0), (0, 0), (0, 0)))
    got_row = passed_along(as_sent(remain[:, :, 0:1, :]), "gy", -1)
    remain = remain[:, :, 1:, :]
    return remain + jnp.pad(got_row, ((0, 0), (0, 0), (remain.shape[2] - 1, 0), (0, 0)))


def input_grad(kernel, errors, extended):
    kernel_f = kernel.astype(jnp.float32)
    _, pullback = jax.vjp(lambda values: exact_conv(values, kernel_f), extended.astype(jnp.float32))
    grid = pullback(errors.astype(jnp.float32))[0]
    return return_rims(grid[:, :, :, 1:])


def weight_grad(errors, extended, kernel):
    source_f = extended.astype(jnp.float32)
    _, pullback = jax.vjp(lambda weights: exact_conv(source_f, weights), kernel.astype(jnp.float32))
    return pullback(errors.astype(jnp.float32))[0]


def local(volume, conv_one, conv_two, conv_three, head_weight, targets):
    inputs = volume[0].astype(jnp.bfloat16)
    ext_one, pre_one = forward_layer(inputs, conv_one)
    act_one = activate(pre_one).astype(jnp.bfloat16)
    ext_two, pre_two = forward_layer(act_one, conv_two)
    act_two = activate(pre_two).astype(jnp.bfloat16)
    ext_three, pre_three = forward_layer(act_two, conv_three)
    act_three = activate(pre_three).astype(jnp.bfloat16)
    local_cells = pre_three.shape[1] * pre_three.shape[2] * pre_three.shape[3]
    cell_count = local_cells * lax.axis_size("gz") * lax.axis_size("gy")
    channel_sums = jnp.sum(act_three.astype(jnp.float32), axis=(1, 2, 3))
    pooled = summed_over_volume(channel_sums) / cell_count
    predicted = jnp.dot(head_weight, pooled, precision=highest)
    errors = predicted - targets[0]
    leader = (lax.axis_index("gz") == 0) & (lax.axis_index("gy") == 0)
    weight_share = jnp.where(leader, 1.0, 0.0).astype(jnp.float32)
    loss_term = weight_share * (0.5 * jnp.sum(errors * errors))
    head_term = weight_share * jnp.outer(errors, pooled)
    back_pool = jnp.dot(errors, head_weight, precision=highest) / cell_count
    err_three = (back_pool[:, None, None, None] * slope_of(pre_three)).astype(jnp.bfloat16)
    grad_three = weight_grad(err_three, ext_three, conv_three)
    back_two = input_grad(conv_three, err_three, ext_three)
    err_two = (back_two * slope_of(pre_two)).astype(jnp.bfloat16)
    grad_two = weight_grad(err_two, ext_two, conv_two)
    back_one = input_grad(conv_two, err_two, ext_two)
    err_one = (back_one * slope_of(pre_one)).astype(jnp.bfloat16)
    grad_one = weight_grad(err_one, ext_one, conv_one)
    head_sum, three_sum, two_sum, one_sum, total_loss = summed_over_all(
        (head_term, grad_three, grad_two, grad_one, loss_term)
    )
    return (
        normalized(one_sum),
        normalized(two_sum),
        normalized(three_sum),
        normalized(head_sum),
        total_loss,
    )


def solution(mesh):
    in_specs = (P("batch", None, "gz", "gy", None), P(), P(), P(), P(), P("batch", None))
    out_specs = (P(), P(), P(), P(), P())
    return jax.shard_map(local, mesh=mesh, in_specs=in_specs, out_specs=out_specs, check_vma=False)
```

```python
import functools
import jax
import jax.numpy as jnp
from jax import lax
from jax.experimental import pallas as pl
from jax.experimental.pallas import tpu as pltpu
from jax.sharding import PartitionSpec as P

epsilon = 1e-06
f32 = jnp.float32
bf16 = jnp.bfloat16
LANES = 128
HALF = 64
G3, G2, G1, GH, GL, ROWS = 0, 448, 560, 592, 600, 640


def call(body, outs, args, scratch=()):
    return pl.pallas_call(
        body,
        out_shape=[jax.ShapeDtypeStruct(s, d) for s, d in outs],
        in_specs=[pl.BlockSpec(memory_space=pltpu.VMEM)] * len(args),
        out_specs=[pl.BlockSpec(memory_space=pltpu.VMEM)] * len(outs),
        scratch_shapes=[pltpu.VMEM(s, d) for s, d in scratch],
        compiler_params=pltpu.CompilerParams(vmem_limit_bytes=48 * 1024 * 1024),
    )(*args)


def lane_of(shape):
    return lax.broadcasted_iota(jnp.int32, shape, len(shape) - 1)


def dot(a, b):
    return lax.dot_general(a, b, (((1,), (0,)), ((), ())), preferred_element_type=f32)


def dot_nt(a, b):
    return lax.dot_general(a, b, (((1,), (1,)), ((), ())), preferred_element_type=f32)


def from_below(own, received):
    mixed = jnp.where(lane_of(own.shape) >= HALF, received.astype(f32), own.astype(f32))
    return pltpu.roll(mixed, HALF, 1)


def from_above(own, received):
    mixed = jnp.where(lane_of(own.shape) < HALF, received.astype(f32), own.astype(f32))
    return pltpu.roll(mixed, HALF, 1)


def x_before(rows):
    return jnp.where(lane_of(rows.shape) % HALF == 0, 0.0, pltpu.roll(rows, 1, 1))


def x_after(rows):
    return jnp.where(lane_of(rows.shape) % HALF == HALF - 1, 0.0, pltpu.roll(rows, LANES - 1, 1))


def at(group):
    return slice(group * LANES, (group + 1) * LANES)


def arrange_body(vol, a0, row, plane, corner, rows):
    for z in range(8):
        tops = [c * 128 + z * 16 + yb * 8 for yb in range(2) for c in range(4)]
        cube = jnp.stack([vol[top : top + 8, :] for top in tops], axis=0)
        rows[z * 64 : z * 64 + 64, :] = jnp.transpose(cube, (1, 0, 2)).reshape(64, 512)
    x_at = lax.broadcasted_iota(jnp.int32, (512, 512), 0)
    to = lax.broadcasted_iota(jnp.int32, (512, 512), 1)
    move = jnp.where(x_at == (to % HALF) * 8 + to // HALF, 1.0, 0.0).astype(bf16)
    phased = dot(rows[...].astype(bf16), move)
    parts = []
    for j in range(4):
        part = phased[:, at(j)].reshape(64, 8, LANES)
        turned = pltpu.roll(pltpu.roll(part, 4, 1), HALF, 2)
        sub = lax.broadcasted_iota(jnp.int32, part.shape, 1)
        parts.append(jnp.where((sub < 4) == (lane_of(part.shape) < HALF), part, turned))
    whole = jnp.concatenate(parts, axis=1).astype(bf16)
    a0[...] = whole.reshape(8, 8, 32, LANES)
    for z in range(8):
        row[z] = a0[z, 7]
    plane[...] = a0[7]
    corner[...] = a0[7, 7]


def weights_body(w1, w2, w3, t1, t2, t3, tt2, tt3):
    eye = jnp.where(
        lax.broadcasted_iota(jnp.int32, (HALF, LANES), 0) == lane_of((HALF, LANES)), 1.0, 0.0
    ).astype(bf16)
    blocks = []
    for ab in range(9):
        both, low = w1[ab, 0], w1[ab, 1]
        for m in range(4):
            block = pltpu.roll(both, 16 * m, 1) if m else both
            if m < 3:
                block = block + pltpu.roll(low, 16 * (m + 1), 1)
            blocks.append(block)
        blocks += [jnp.zeros_like(low), low]
    t1[...] = dot_nt(eye, jnp.concatenate(blocks, axis=0).astype(bf16)).astype(bf16)
    blocks = []
    for ab in range(9):
        e0, e1, e2 = w2[3 * ab], w2[3 * ab + 1], w2[3 * ab + 2]
        blocks += [e1, e2 + pltpu.roll(e0, 32, 1), pltpu.roll(e1, 32, 1), pltpu.roll(e2, 32, 1), e0]
    tt2[...] = jnp.concatenate(blocks, axis=0).astype(bf16)
    t2[...] = dot_nt(eye, tt2[...]).astype(bf16)
    blocks = []
    for ab in range(9):
        blocks += [w3[3 * ab + 1], w3[3 * ab + 2], w3[3 * ab]]
    tt3[...] = jnp.concatenate(blocks, axis=0).astype(bf16)
    t3[...] = dot_nt(eye, tt3[...]).astype(bf16)


def fill_patches(tile, n, rows, moved, out):
    step, groups = rows + moved, n // 2
    for zz in range(-1, n):
        for yy in range(-1, n):
            cell = tile(zz, yy)
            shifted = x_before(cell[rows - moved :].astype(f32)).astype(bf16)
            for a in range(3):
                for b in range(3):
                    i, j = zz + 1 - a, yy + 1 - b
                    if i % 2 or j % 2 or not (0 <= i < n and 0 <= j < n):
                        continue
                    top = (a * 3 + b) * step
                    g = at((i // 2) * groups + j // 2)
                    out[top : top + rows, g] = cell
                    out[top + rows : top + step, g] = shifted


def finish(pre):
    root = jnp.sqrt(pre * pre + 1.0)
    return 0.65 * pre + 0.35 * (root - 1.0), 0.65 + 0.35 * pre / root


def one_body(a0, row, plane, corner, t1, p1, a1, slope, row_out, plane_out, corner_out):
    def tile(zz, yy):
        own = a0[zz, yy if yy >= 0 else 7] if zz >= 0 else plane[yy if yy >= 0 else 7]
        if yy >= 0:
            return own
        return from_below(own, row[zz] if zz >= 0 else corner[...]).astype(bf16)

    fill_patches(tile, 8, 32, 16, p1)
    act, slope[...] = finish(dot(t1[...], p1[...]))
    a1[...] = act.astype(bf16)
    for z in range(4):
        row_out[:, at(z)] = a1[:, at(z * 4 + 3)]
    plane_out[...] = a1[:, 12 * LANES :]
    corner_out[...] = a1[:, at(15)]


def two_body(a1, row, plane, corner, t2, p2, a2, slope, row_out, plane_out, corner_out):
    def tile(zz, yy):
        y_own = yy if yy >= 0 else 3
        own = a1[:, at(zz * 4 + y_own)] if zz >= 0 else plane[:, at(y_own)]
        if yy >= 0:
            return own
        return from_below(own, row[:, at(zz)] if zz >= 0 else corner[...]).astype(bf16)

    fill_patches(tile, 4, 64, 16, p2)
    act, slope[...] = finish(dot(t2[...], p2[...]))
    a2[...] = act.astype(bf16)
    for z in range(2):
        row_out[:, at(z)] = a2[:, at(z * 2 + 1)]
    plane_out[...] = a2[:, 2 * LANES :]
    corner_out[...] = a2[:, at(3)]


def three_body(a2, row, plane, corner, t3, slope2, p3, slope, sums, to_z, to_y, to_corner):
    def tile(zz, yy):
        y_own = yy if yy >= 0 else 1
        own = a2[:, at(zz * 2 + y_own)] if zz >= 0 else plane[:, at(y_own)]
        if yy >= 0:
            return own
        return from_below(own, row[:, at(zz)] if zz >= 0 else corner[...]).astype(bf16)

    fill_patches(tile, 2, 64, 32, p3)
    act, slope3 = finish(dot(t3[...], p3[...]))
    slope[...] = slope3
    column = jnp.sum(act.astype(bf16).astype(f32), axis=1, keepdims=True)
    spot = lax.broadcasted_iota(jnp.int32, (HALF, LANES), 0) == lane_of((HALF, LANES))
    line = jnp.sum(jnp.where(spot, column, 0.0), axis=0, keepdims=True)
    sums[...] = jnp.broadcast_to(line, sums.shape)
    third = slope3.astype(bf16)
    second = slope2[...].astype(bf16)
    to_z[:, : 2 * LANES] = second[:, : 2 * LANES]
    to_z[:, 2 * LANES :] = third
    to_y[:, at(0)] = second[:, at(0)]
    to_y[:, at(1)] = second[:, at(2)]
    to_y[:, at(2)] = third
    to_corner[:, at(0)] = second[:, at(0)]
    to_corner[:, at(1)] = third


def reach(index):
    return [(1, index // 2)] if index % 2 == 0 else [(2, index // 2), (0, index // 2 + 1)]


def back_cell(terms, z, y, step, rows, place):
    total = None
    for a, i in reach(z):
        for b, j in reach(y):
            top = (a * 3 + b) * step
            part = terms[top : top + step, at(place(i, j))]
            total = part if total is None else total + part
    moved = step - rows
    low = total[rows - moved : rows] + x_after(total[rows:])
    return jnp.concatenate([total[: rows - moved], low], axis=0)


def backward_body(cells, share, gathered, head, targets, s1, s2, s3, of_z, of_y, of_corner,
                  p1, p2, p3, tt2, tt3, out, err3, err2, err1, terms3, terms2):
    out[...] = jnp.zeros_like(out)
    pooled = jnp.sum(gathered[...], axis=0, keepdims=True)[:, :HALF] / cells
    errors = jnp.sum(head[...] * pooled, axis=1, keepdims=True) - targets[...]
    out[GH : GH + 4, :HALF] = errors * pooled * share
    loss = 0.5 * jnp.sum(errors * errors, axis=0, keepdims=True) * share
    out[GL : GL + 1, :] = jnp.broadcast_to(loss, (1, LANES))
    line = jnp.sum(errors * head[...], axis=0, keepdims=True) / cells
    spot = lax.broadcasted_iota(jnp.int32, (HALF, HALF), 0) == lane_of((HALF, HALF))
    back_pool = jnp.sum(jnp.where(spot, line, 0.0), axis=1, keepdims=True)

    third, third_z = s3[...], of_z[:, at(2)].astype(f32)
    slopes3 = [third, from_above(third, of_y[:, at(2)]),
               third_z, from_above(third_z, of_corner[:, at(1)])]
    for k in range(4):
        err3[:HALF, at(k)] = (back_pool * slopes3[k]).astype(bf16)
    err3[HALF:, :] = jnp.zeros((HALF, 4 * LANES), bf16)
    err2[HALF:, :] = jnp.zeros((HALF, 9 * LANES), bf16)
    err1[HALF:, :] = jnp.zeros((HALF, 16 * LANES), bf16)

    terms3[...] = dot(tt3[...], err3[...])
    order = [(0, 0), (0, 1), (1, 0), (1, 1), (0, 2), (1, 2), (2, 0), (2, 1), (2, 2)]
    for k, (z, y) in enumerate(order):
        if z < 2:
            own = s2[:, at(z * 2 + (y if y < 2 else 0))]
            slope = own if y < 2 else from_above(own, of_y[:, at(z)])
        else:
            own = of_z[:, at(y if y < 2 else 0)].astype(f32)
            slope = own if y < 2 else from_above(own, of_corner[:, at(0)])
        back = back_cell(terms3, z, y, 96, 64, lambda i, j: i * 2 + j)
        err2[:HALF, at(k)] = (back * slope).astype(bf16)

    terms2[...] = dot(tt2[...], err2[...])
    for z in range(4):
        for y in range(4):
            back = back_cell(terms2, z, y, 80, 64, lambda i, j: order.index((i, j)))
            k = at(z * 4 + y)
            err1[:HALF, k] = (back * s1[:, k]).astype(bf16)

    grad = dot_nt(p3[...], err3[:, at(0)])
    taps = [96 * ab + 32 * ((e + 2) % 3) for ab in range(9) for e in range(3)]
    for k, top in enumerate(taps[:14]):
        block = grad[top : top + 32]
        if k + 14 < 27:
            other = taps[k + 14]
            block = block + pltpu.roll(grad[other : other + 32], HALF, 1)
        out[G3 + 32 * k : G3 + 32 * k + 32, :] = block

    grad = dot_nt(p2[...], err2[:, : 4 * LANES])
    blocks = []
    for ab in range(9):
        x = [grad[80 * ab + 16 * i : 80 * ab + 16 * i + 16] for i in range(5)]
        for first, second in ((4, 1), (0, 2), (1, 3)):
            block = x[first] + pltpu.roll(x[second], LANES - 32, 1)
            blocks.append(jnp.where(lane_of(block.shape) < 32, block, 0.0))
    for k in range(7):
        block = blocks[k]
        for m in range(1, 4):
            if k + 7 * m < 27:
                block = block + pltpu.roll(blocks[k + 7 * m], 32 * m, 1)
        out[G2 + 16 * k : G2 + 16 * k + 16, :] = block

    grad = dot_nt(p1[...], err1[...])
    blocks = []
    for ab in range(9):
        x = [grad[48 * ab + 8 * i : 48 * ab + 8 * i + 8] for i in range(6)]
        both, low = x[0], x[5]
        for m in range(1, 4):
            both = both + pltpu.roll(x[m], LANES - 16 * m, 1)
            low = low + pltpu.roll(x[m - 1], LANES - 16 * m, 1)
        low = jnp.where(lax.broadcasted_iota(jnp.int32, low.shape, 0) >= 4, low, 0.0)
        block = jnp.concatenate([both, low], axis=0)
        blocks.append(jnp.where(lane_of(block.shape) < 16, block, 0.0))
    block = blocks[0]
    for m in range(1, 8):
        block = block + pltpu.roll(blocks[m], 16 * m, 1)
    out[G1 : G1 + 16, :] = block
    out[G1 + 16 : G1 + 32, :] = blocks[8]


def update_body(total, u1, u2, u3, uh, loss):
    def scale(start, stop, count):
        squares = total[start:stop] * total[start:stop]
        mean = jnp.sum(jnp.sum(squares, axis=0, keepdims=True), axis=1, keepdims=True) / count
        return 1.0 / jnp.sqrt(mean + epsilon)

    factor = scale(G3, G2, 64 * 32 * 27)
    for k in range(14):
        block = total[G3 + 32 * k : G3 + 32 * k + 32] * factor
        u3[k] = block[:, :HALF]
        if k + 14 < 27:
            u3[k + 14] = pltpu.roll(block, HALF, 1)[:, :HALF]
    factor = scale(G2, G1, 32 * 16 * 27)
    for k in range(7):
        block = total[G2 + 16 * k : G2 + 16 * k + 16] * factor
        for m in range(4):
            if k + 7 * m < 27:
                u2[k + 7 * m] = (pltpu.roll(block, LANES - 32 * m, 1) if m else block)[:, :32]
    factor = scale(G1, GH, 16 * 4 * 27)
    for ab in range(9):
        m = ab % 8
        block = total[G1 + 16 * (ab // 8) : G1 + 16 * (ab // 8) + 16] * factor
        block = (pltpu.roll(block, LANES - 16 * m, 1) if m else block)[:, :16]
        u1[3 * ab] = block[12:16]
        u1[3 * ab + 1] = block[0:4]
        u1[3 * ab + 2] = block[4:8]
    uh[...] = total[GH : GH + 4, :HALF] * scale(GH, GL, 4 * 64)
    loss[...] = total[GL : GL + 1, :]


def neighbours(by):
    gz, gy = lax.axis_size("gz"), lax.axis_size("gy")
    z = [(i, i + by) for i in range(gz) if 0 <= i + by < gz]
    y = [(i, i + by) for i in range(gy) if 0 <= i + by < gy]
    corner = [(i * gy + j, k * gy + l) for i, k in z for j, l in y]
    return y, z, corner


def exchange(row, plane, corner, by):
    y, z, both = neighbours(by)
    return (lax.ppermute(row, "gy", y), lax.ppermute(plane, "gz", z),
            lax.ppermute(corner, ("gz", "gy"), both))


def gathered(x, axes):
    count = lax.axis_size(axes)
    return lax.all_to_all(jnp.broadcast_to(x[None], (count,) + x.shape), axes, 0, 0)


def summed_over_all(flat):
    columns = lax.axis_size("gy")
    flat = flat.reshape(columns, ROWS // columns, LANES)
    own = jnp.sum(lax.all_to_all(flat, "gy", 0, 0), axis=0)
    own = lax.psum(own, "batch")
    own = jnp.sum(gathered(own, "gz"), axis=0)
    return gathered(own, "gy").reshape(ROWS, LANES)


def local(volume, conv_one, conv_two, conv_three, head_weight, targets):
    devices = lax.axis_size("gz") * lax.axis_size("gy")
    cells = float(devices * LANES)

    def taps(w):
        w = jnp.transpose(w, (2, 3, 4, 1, 0)).astype(f32)
        return jnp.pad(w.reshape((27,) + w.shape[3:]), ((0, 0), (0, 0), (0, LANES - w.shape[4])))

    w1 = taps(conv_one).reshape(9, 3, 4, LANES)
    both = w1[:, 1:].reshape(9, 1, 8, LANES)
    low = jnp.pad(w1[:, :1], ((0, 0), (0, 0), (4, 0), (0, 0)))
    t1, t2, t3, tt2, tt3 = call(
        weights_body,
        [((64, 432), bf16), ((64, 720), bf16), ((64, 864), bf16), ((720, LANES), bf16), ((864, LANES), bf16)],
        (jnp.concatenate([both, low], axis=1), taps(conv_two), taps(conv_three)),
    )
    a0, row, plane, corner = call(
        arrange_body,
        [((8, 8, 32, LANES), bf16), ((8, 32, LANES), bf16), ((8, 32, LANES), bf16), ((32, LANES), bf16)],
        (volume.reshape(512, 512),),
        [((512, 512), f32)],
    )
    row, plane, corner = exchange(row, plane, corner, 1)
    p1, a1, s1, row, plane, corner = call(
        one_body,
        [((432, 2048), bf16), ((64, 2048), bf16), ((64, 2048), f32),
         ((64, 512), bf16), ((64, 512), bf16), ((64, LANES), bf16)],
        (a0, row, plane, corner, t1),
    )
    row, plane, corner = exchange(row, plane, corner, 1)
    p2, a2, s2, row, plane, corner = call(
        two_body,
        [((720, 512), bf16), ((64, 512), bf16), ((64, 512), f32),
         ((64, 256), bf16), ((64, 256), bf16), ((64, LANES), bf16)],
        (a1, row, plane, corner, t2),
    )
    row, plane, corner = exchange(row, plane, corner, 1)
    p3, s3, sums, to_z, to_y, to_corner = call(
        three_body,
        [((864, LANES), bf16), ((64, LANES), f32), ((devices, LANES), f32),
         ((64, 384), bf16), ((64, 384), bf16), ((64, 256), bf16)],
        (a2, row, plane, corner, t3, s2),
    )
    of_y, of_z, of_corner = exchange(to_y, to_z, to_corner, -1)
    pooled = lax.all_to_all(sums, ("gz", "gy"), 0, 0, tiled=True)
    (flat,) = call(
        functools.partial(backward_body, cells, 1.0 / devices),
        [((ROWS, LANES), f32)],
        (pooled, head_weight, targets.reshape(4, 1), s1, s2, s3, of_z, of_y, of_corner, p1, p2, p3, tt2, tt3),
        [((LANES, 4 * LANES), bf16), ((LANES, 9 * LANES), bf16), ((LANES, 16 * LANES), bf16),
         ((864, 4 * LANES), f32), ((720, 9 * LANES), f32)],
    )
    u1, u2, u3, uh, loss = call(
        update_body,
        [((27, 4, 16), f32), ((27, 16, 32), f32), ((27, 32, 64), f32), ((4, 64), f32), ((1, LANES), f32)],
        (summed_over_all(flat),),
    )

    def kernel_form(u):
        return jnp.transpose(u.reshape((3, 3, 3) + u.shape[1:]), (4, 3, 0, 1, 2))

    return kernel_form(u1), kernel_form(u2), kernel_form(u3), uh, loss[0, 0]


def solution(mesh):
    in_specs = (P("batch", None, "gz", "gy", None), P(), P(), P(), P(), P("batch", None))
    out_specs = (P(), P(), P(), P(), P())
    return jax.shard_map(local, mesh=mesh, in_specs=in_specs, out_specs=out_specs, check_vma=False)
```

```python
import functools
import jax
import jax.numpy as jnp
from jax import lax
from jax.experimental import pallas as pl
from jax.experimental.pallas import tpu as pltpu
from jax.sharding import PartitionSpec as P

epsilon = 1e-06
f32 = jnp.float32
bf16 = jnp.bfloat16
LANES = 128
HALF = 64
CHUNKS, ROWS, HIGH, LOW = 16, 48, 40, 41


def call(body, outs, args, scratch=()):
    return pl.pallas_call(
        body,
        out_shape=[jax.ShapeDtypeStruct(s, d) for s, d in outs],
        in_specs=[pl.BlockSpec(memory_space=pltpu.VMEM)] * len(args),
        out_specs=[pl.BlockSpec(memory_space=pltpu.VMEM)] * len(outs),
        scratch_shapes=[pltpu.VMEM(s, d) for s, d in scratch],
        compiler_params=pltpu.CompilerParams(vmem_limit_bytes=48 * 1024 * 1024),
    )(*args)


def lane_of(shape):
    return lax.broadcasted_iota(jnp.int32, shape, len(shape) - 1)


def dot(a, b):
    return lax.dot_general(a, b, (((1,), (0,)), ((), ())), preferred_element_type=f32)


def dot_nt(a, b):
    return lax.dot_general(a, b, (((1,), (1,)), ((), ())), preferred_element_type=f32)


def upper_half(tile):
    top, bottom = tile[:16].astype(f32), tile[16:].astype(f32)
    return jnp.where(lane_of(top.shape) < HALF, pltpu.roll(top, HALF, 1), bottom).astype(bf16)


def row_below(own, received):
    turned, got = pltpu.roll(own.astype(f32), HALF, 1), received.astype(f32)
    low = lane_of(got.shape) < HALF
    top = jnp.where(low, got, turned[:16])
    bottom = jnp.where(low, pltpu.roll(got, HALF, 1), turned[16:])
    return jnp.concatenate([top, bottom], axis=0).astype(bf16)


def x_before(rows):
    return jnp.where(lane_of(rows.shape) % HALF == 0, 0.0, pltpu.roll(rows, 1, 1))


def x_after(rows):
    return jnp.where(lane_of(rows.shape) % HALF == HALF - 1, 0.0, pltpu.roll(rows, LANES - 1, 1))


def at(group):
    return slice(group * LANES, (group + 1) * LANES)


def arrange_body(vol, a0, row, plane, corner, rows):
    for z in range(8):
        tops = [c * 128 + z * 16 + yb * 8 for yb in range(2) for c in range(4)]
        cube = jnp.stack([vol[top : top + 8, :] for top in tops], axis=0)
        rows[z * 64 : z * 64 + 64, :] = jnp.transpose(cube, (1, 0, 2)).reshape(64, 512)
    x_at = lax.broadcasted_iota(jnp.int32, (512, 512), 0)
    to = lax.broadcasted_iota(jnp.int32, (512, 512), 1)
    move = jnp.where(x_at == (to % HALF) * 8 + to // HALF, 1.0, 0.0).astype(bf16)
    phased = dot(rows[...].astype(bf16), move)
    parts = []
    for j in range(4):
        part = phased[:, at(j)].reshape(64, 8, LANES)
        turned = pltpu.roll(pltpu.roll(part, 4, 1), HALF, 2)
        sub = lax.broadcasted_iota(jnp.int32, part.shape, 1)
        parts.append(jnp.where((sub < 4) == (lane_of(part.shape) < HALF), part, turned))
    whole = jnp.concatenate(parts, axis=1).astype(bf16)
    a0[...] = whole.reshape(8, 8, 32, LANES)
    plane[...] = a0[1:]
    for z in range(8):
        for yp in range(1, 8):
            half = upper_half(a0[z, yp])
            row[z, 16 * yp - 16 : 16 * yp, :] = half
            if z > 0:
                corner[z - 1, 16 * yp - 16 : 16 * yp, :] = half


def weights_body(w1, w2, w3, t1, t2, t3, tt2, tt3):
    eye = jnp.where(
        lax.broadcasted_iota(jnp.int32, (HALF, LANES), 0) == lane_of((HALF, LANES)), 1.0, 0.0
    ).astype(bf16)
    blocks = []
    for ab in range(9):
        both, low = w1[ab, 0], w1[ab, 1]
        for m in range(4):
            block = pltpu.roll(both, 16 * m, 1) if m else both
            if m < 3:
                block = block + pltpu.roll(low, 16 * (m + 1), 1)
            blocks.append(block)
        blocks += [jnp.zeros_like(low), low]
    t1[...] = dot_nt(eye, jnp.concatenate(blocks, axis=0).astype(bf16)).astype(bf16)
    blocks = []
    for ab in range(9):
        e0, e1, e2 = w2[3 * ab], w2[3 * ab + 1], w2[3 * ab + 2]
        blocks += [e1, e2 + pltpu.roll(e0, 32, 1), pltpu.roll(e1, 32, 1), pltpu.roll(e2, 32, 1), e0]
    tt2[...] = jnp.concatenate(blocks, axis=0).astype(bf16)
    t2[...] = dot_nt(eye, tt2[...]).astype(bf16)
    blocks = []
    for ab in range(9):
        blocks += [w3[3 * ab + 1], w3[3 * ab + 2], w3[3 * ab]]
    tt3[...] = jnp.concatenate(blocks, axis=0).astype(bf16)
    t3[...] = dot_nt(eye, tt3[...]).astype(bf16)


def fill_patches(tile, low, high, rows, moved, out):
    step, count = rows + moved, high - low + 1
    for zz in range(2 * low - 1, 2 * high + 2):
        for yy in range(2 * low - 1, 2 * high + 2):
            cell = tile(zz, yy)
            shifted = x_before(cell[rows - moved :].astype(f32)).astype(bf16)
            for a in range(3):
                for b in range(3):
                    i, j = zz + 1 - a, yy + 1 - b
                    if i % 2 or j % 2:
                        continue
                    i, j = i // 2 - low, j // 2 - low
                    if not (0 <= i < count and 0 <= j < count):
                        continue
                    top = (a * 3 + b) * step
                    out[top : top + rows, at(i * count + j)] = cell
                    out[top + rows : top + step, at(i * count + j)] = shifted


def finish(pre):
    root = jnp.sqrt(pre * pre + 1.0)
    return 0.65 * pre + 0.35 * (root - 1.0), 0.65 + 0.35 * pre / root


def forward_body(a0, row, plane, corner, t1, t2, t3, p1, p2, p3, s1, s2, s3, sums, a1, a2):
    def tile_one(zz, yy):
        own = a0[zz, yy % 8] if zz >= 0 else plane[zz + 7, yy % 8]
        if yy >= 0:
            return own
        part = slice(16 * (yy + 7), 16 * (yy + 8))
        return row_below(own, row[zz, part, :] if zz >= 0 else corner[zz + 7, part, :])

    fill_patches(tile_one, -3, 3, 32, 16, p1)
    act, s1[...] = finish(dot(t1[...], p1[...]))
    a1[...] = act.astype(bf16)
    fill_patches(lambda z, y: a1[:, at((z + 3) * 7 + y + 3)], -1, 1, 64, 16, p2)
    act, s2[...] = finish(dot(t2[...], p2[...]))
    a2[...] = act.astype(bf16)
    fill_patches(lambda z, y: a2[:, at((z + 1) * 3 + y + 1)], 0, 0, 64, 32, p3)
    act, s3[...] = finish(dot(t3[...], p3[...]))
    column = jnp.sum(act.astype(bf16).astype(f32), axis=1, keepdims=True)
    spot = lax.broadcasted_iota(jnp.int32, (HALF, LANES), 0) == lane_of((HALF, LANES))
    line = jnp.sum(jnp.where(spot, column, 0.0), axis=0, keepdims=True)
    sums[...] = jnp.broadcast_to(line, sums.shape)


def reach(index):
    return [(1, index // 2)] if index % 2 == 0 else [(2, index // 2), (0, index // 2 + 1)]


def back_cell(terms, z, y, step, rows, low, high):
    total = None
    for a, i in reach(z):
        for b, j in reach(y):
            if low <= i <= high and low <= j <= high:
                top = (a * 3 + b) * step
                part = terms[top : top + step, at((i - low) * (high - low + 1) + j - low)]
                total = part if total is None else total + part
    moved = step - rows
    last = total[rows - moved : rows] + x_after(total[rows:])
    return jnp.concatenate([total[: rows - moved], last], axis=0)


def backward_body(cells, share, gathered, head, targets, s1, s2, s3, p1, p2, p3, tt2, tt3,
                  result, out, err3, err2, err1, terms3, terms2):
    out[...] = jnp.zeros_like(out)
    pooled = jnp.sum(gathered[...], axis=0, keepdims=True)[:, :HALF] / cells
    errors = jnp.sum(head[...] * pooled, axis=1, keepdims=True) - targets[...]
    outer = errors * pooled * share
    loss = 0.5 * jnp.sum(errors * errors, axis=0, keepdims=True) * share
    exact = [jnp.concatenate([outer[0:1], outer[1:2]], axis=1),
             jnp.concatenate([outer[2:3], outer[3:4]], axis=1),
             jnp.broadcast_to(loss, (1, LANES))]
    for k, value in enumerate(exact):
        first = value.astype(bf16).astype(f32)
        out[k, HIGH : HIGH + 1, :] = first
        out[k, LOW : LOW + 1, :] = value - first
    line = jnp.sum(errors * head[...], axis=0, keepdims=True) / cells
    spot = lax.broadcasted_iota(jnp.int32, (HALF, HALF), 0) == lane_of((HALF, HALF))
    back_pool = jnp.sum(jnp.where(spot, line, 0.0), axis=1, keepdims=True)

    err3[:HALF, :] = (back_pool * s3[...]).astype(bf16)
    err3[HALF:, :] = jnp.zeros((HALF, LANES), bf16)
    err2[HALF:, :] = jnp.zeros((HALF, 9 * LANES), bf16)
    err1[HALF:, :] = jnp.zeros((HALF, 49 * LANES), bf16)
    terms3[...] = dot(tt3[...], err3[...])
    for k in range(9):
        back = back_cell(terms3, k // 3 - 1, k % 3 - 1, 96, 64, 0, 0)
        err2[:HALF, at(k)] = (back * s2[:, at(k)]).astype(bf16)
    terms2[...] = dot(tt2[...], err2[...])
    for k in range(49):
        back = back_cell(terms2, k // 7 - 3, k % 7 - 3, 80, 64, -1, 1)
        err1[:HALF, at(k)] = (back * s1[:, at(k)]).astype(bf16)

    grad = dot_nt(p3[...], err3[...])
    taps = [96 * ab + 32 * ((e + 2) % 3) for ab in range(9) for e in range(3)]
    for k, top in enumerate(taps[:14]):
        block = grad[top : top + 32]
        if k + 14 < 27:
            other = taps[k + 14]
            block = block + pltpu.roll(grad[other : other + 32], HALF, 1)
        out[k, :32, :] = block

    grad = dot_nt(p2[...], err2[...])
    blocks = []
    for ab in range(9):
        x = [grad[80 * ab + 16 * i : 80 * ab + 16 * i + 16] for i in range(5)]
        for first, second in ((4, 1), (0, 2), (1, 3)):
            block = x[first] + pltpu.roll(x[second], LANES - 32, 1)
            blocks.append(jnp.where(lane_of(block.shape) < 32, block, 0.0))
    for k in range(7):
        block = blocks[k]
        for m in range(1, 4):
            if k + 7 * m < 27:
                block = block + pltpu.roll(blocks[k + 7 * m], 32 * m, 1)
        for i, (chunk, top) in enumerate(places_two(k)):
            out[chunk, top : top + 8, :] = block[8 * i : 8 * i + 8]

    grad = dot_nt(p1[...], err1[...])
    blocks = []
    for ab in range(9):
        x = [grad[48 * ab + 8 * i : 48 * ab + 8 * i + 8] for i in range(6)]
        both, low = x[0], x[5]
        for m in range(1, 4):
            both = both + pltpu.roll(x[m], LANES - 16 * m, 1)
            low = low + pltpu.roll(x[m - 1], LANES - 16 * m, 1)
        low = jnp.where(lax.broadcasted_iota(jnp.int32, low.shape, 0) >= 4, low, 0.0)
        block = jnp.concatenate([both, low], axis=0)
        blocks.append(jnp.where(lane_of(block.shape) < 16, block, 0.0))
    block = blocks[0]
    for m in range(1, 8):
        block = block + pltpu.roll(blocks[m], 16 * m, 1)
    for m, block in enumerate((block, blocks[8])):
        for i, (chunk, top) in enumerate(places_one(m)):
            out[chunk, top : top + 8, :] = block[8 * i : 8 * i + 8]
    result[...] = out[...].astype(bf16)


def places_two(k):
    if k < 4:
        return [(14 + k // 2, 16 * (k % 2)), (14 + k // 2, 16 * (k % 2) + 8)]
    return [(2 * k - 8, 32), (2 * k - 7, 32)]


def places_one(m):
    return [(6 + 2 * m, 32), (7 + 2 * m, 32)]


def total_body(parts, out):
    total = parts[0].astype(f32)
    for k in range(1, parts.shape[0]):
        total = total + parts[k].astype(f32)
    exact = total[HIGH : HIGH + 1] + total[LOW : LOW + 1]
    first = exact.astype(bf16).astype(f32)
    at_row = lax.broadcasted_iota(jnp.int32, total.shape, 0)
    total = jnp.where(at_row == HIGH, first, jnp.where(at_row == LOW, exact - first, total))
    total = total.astype(bf16)
    for k in range(out.shape[0]):
        out[k] = total


def update_body(sent, u1, u2, u3, uh, loss, total):
    total[...] = sent[...].astype(f32)

    def scale(blocks, count):
        mean = 0.0
        for block in blocks:
            squares = jnp.sum(block * block, axis=0, keepdims=True)
            mean = mean + jnp.sum(squares, axis=1, keepdims=True) / count
        return 1.0 / jnp.sqrt(mean + epsilon)

    def read(places):
        return jnp.concatenate([total[chunk, top : top + 8, :] for chunk, top in places], axis=0)

    blocks = [total[k, :32, :] for k in range(14)]
    factor = scale(blocks, 64 * 32 * 27)
    for k, block in enumerate(blocks):
        block = block * factor
        u3[k] = block[:, :HALF]
        if k + 14 < 27:
            u3[k + 14] = pltpu.roll(block, HALF, 1)[:, :HALF]
    blocks = [read(places_two(k)) for k in range(7)]
    factor = scale(blocks, 32 * 16 * 27)
    for k, block in enumerate(blocks):
        block = block * factor
        for m in range(4):
            if k + 7 * m < 27:
                u2[k + 7 * m] = (pltpu.roll(block, LANES - 32 * m, 1) if m else block)[:, :32]
    blocks = [read(places_one(m)) for m in range(2)]
    factor = scale(blocks, 16 * 4 * 27)
    for ab in range(9):
        m = ab % 8
        block = blocks[ab // 8] * factor
        block = (pltpu.roll(block, LANES - 16 * m, 1) if m else block)[:, :16]
        u1[3 * ab] = block[12:16]
        u1[3 * ab + 1] = block[0:4]
        u1[3 * ab + 2] = block[4:8]
    exact = [total[k, HIGH : HIGH + 1, :] + total[k, LOW : LOW + 1, :] for k in range(3)]
    factor = scale(exact[:2], 4 * 64)
    for k in range(2):
        line = exact[k] * factor
        uh[2 * k : 2 * k + 1, :] = line[:, :HALF]
        uh[2 * k + 1 : 2 * k + 2, :] = pltpu.roll(line, HALF, 1)[:, :HALF]
    loss[...] = exact[2]


def neighbours(by):
    gz, gy = lax.axis_size("gz"), lax.axis_size("gy")
    z = [(i, i + by) for i in range(gz) if 0 <= i + by < gz]
    y = [(i, i + by) for i in range(gy) if 0 <= i + by < gy]
    corner = [(i * gy + j, k * gy + l) for i, k in z for j, l in y]
    return y, z, corner


def exchange(row, plane, corner, by):
    y, z, both = neighbours(by)
    return (lax.ppermute(row, "gy", y), lax.ppermute(plane, "gz", z),
            lax.ppermute(corner, ("gz", "gy"), both))


def summed_over_all(parts):
    beyond = lax.axis_size(("batch", "gz"))
    parts = lax.all_to_all(parts, "gy", 0, 0, tiled=True)
    (parts,) = call(total_body, [((beyond, ROWS, LANES), bf16)], (parts,))
    parts = lax.all_to_all(parts, ("batch", "gz"), 0, 0, tiled=True)
    (parts,) = call(total_body, [((CHUNKS, ROWS, LANES), bf16)], (parts,))
    return lax.all_to_all(parts, "gy", 0, 0, tiled=True)


def local(volume, conv_one, conv_two, conv_three, head_weight, targets):
    devices = lax.axis_size("gz") * lax.axis_size("gy")
    cells = float(devices * LANES)

    def taps(w):
        w = jnp.transpose(w, (2, 3, 4, 1, 0)).astype(f32)
        return jnp.pad(w.reshape((27,) + w.shape[3:]), ((0, 0), (0, 0), (0, LANES - w.shape[4])))

    w1 = taps(conv_one).reshape(9, 3, 4, LANES)
    both = w1[:, 1:].reshape(9, 1, 8, LANES)
    low = jnp.pad(w1[:, :1], ((0, 0), (0, 0), (4, 0), (0, 0)))
    t1, t2, t3, tt2, tt3 = call(
        weights_body,
        [((64, 432), bf16), ((64, 720), bf16), ((64, 864), bf16), ((720, LANES), bf16), ((864, LANES), bf16)],
        (jnp.concatenate([both, low], axis=1), taps(conv_two), taps(conv_three)),
    )
    a0, row, plane, corner = call(
        arrange_body,
        [((8, 8, 32, LANES), bf16), ((8, 112, LANES), bf16), ((7, 8, 32, LANES), bf16), ((7, 112, LANES), bf16)],
        (volume.reshape(512, 512),),
        [((512, 512), f32)],
    )
    row, plane, corner = exchange(row, plane, corner, 1)
    p1, p2, p3, s1, s2, s3, sums = call(
        forward_body,
        [((432, 49 * LANES), bf16), ((720, 9 * LANES), bf16), ((864, LANES), bf16),
         ((64, 49 * LANES), f32), ((64, 9 * LANES), f32), ((64, LANES), f32), ((devices, LANES), f32)],
        (a0, row, plane, corner, t1, t2, t3),
        [((64, 49 * LANES), bf16), ((64, 9 * LANES), bf16)],
    )
    pooled = lax.all_to_all(sums, ("gz", "gy"), 0, 0, tiled=True)
    (flat,) = call(
        functools.partial(backward_body, cells, 1.0 / devices),
        [((CHUNKS, ROWS, LANES), bf16)],
        (pooled, head_weight, targets.reshape(4, 1), s1, s2, s3, p1, p2, p3, tt2, tt3),
        [((CHUNKS, ROWS, LANES), f32), ((LANES, LANES), bf16), ((LANES, 9 * LANES), bf16),
         ((LANES, 49 * LANES), bf16), ((864, LANES), f32), ((720, 9 * LANES), f32)],
    )
    u1, u2, u3, uh, loss = call(
        update_body,
        [((27, 4, 16), f32), ((27, 16, 32), f32), ((27, 32, 64), f32), ((4, 64), f32), ((1, LANES), f32)],
        (summed_over_all(flat),),
        [((CHUNKS, ROWS, LANES), f32)],
    )

    def kernel_form(u):
        return jnp.transpose(u.reshape((3, 3, 3) + u.shape[1:]), (4, 3, 0, 1, 2))

    return kernel_form(u1), kernel_form(u2), kernel_form(u3), uh, loss[0, 0]


def solution(mesh):
    in_specs = (P("batch", None, "gz", "gy", None), P(), P(), P(), P(), P("batch", None))
    out_specs = (P(), P(), P(), P(), P())
    return jax.shard_map(local, mesh=mesh, in_specs=in_specs, out_specs=out_specs, check_vma=False)
```

```python
import functools
import jax
import jax.numpy as jnp
from jax import lax
from jax.experimental import pallas as pl
from jax.experimental.pallas import tpu as pltpu
from jax.sharding import PartitionSpec as P

epsilon = 1e-06
f32 = jnp.float32
bf16 = jnp.bfloat16
LANES = 128
HALF = 64
CHUNKS, ROWS, HIGH, LOW = 16, 48, 40, 41
AT_TWO, AT_HEAD = 49 * LANES, 59 * LANES


def call(body, outs, args, scratch=(), mib=8):
    return pl.pallas_call(
        body,
        out_shape=[jax.ShapeDtypeStruct(s, d) for s, d in outs],
        in_specs=[pl.BlockSpec(memory_space=pltpu.VMEM)] * len(args),
        out_specs=[pl.BlockSpec(memory_space=pltpu.VMEM)] * len(outs),
        scratch_shapes=[pltpu.VMEM(s, d) for s, d in scratch],
        compiler_params=pltpu.CompilerParams(vmem_limit_bytes=mib * 1024 * 1024),
    )(*args)


def lane_of(shape):
    return lax.broadcasted_iota(jnp.int32, shape, len(shape) - 1)


def dot(a, b):
    return lax.dot_general(a, b, (((1,), (0,)), ((), ())), preferred_element_type=f32)


def dot_nt(a, b):
    return lax.dot_general(a, b, (((1,), (1,)), ((), ())), preferred_element_type=f32)


def upper_half(tile):
    top, bottom = tile[:16].astype(f32), tile[16:].astype(f32)
    return jnp.where(lane_of(top.shape) < HALF, pltpu.roll(top, HALF, 1), bottom).astype(bf16)


def row_below(own, received):
    turned, got = pltpu.roll(own.astype(f32), HALF, 1), received.astype(f32)
    low = lane_of(got.shape) < HALF
    top = jnp.where(low, got, turned[:16])
    bottom = jnp.where(low, pltpu.roll(got, HALF, 1), turned[16:])
    return jnp.concatenate([top, bottom], axis=0).astype(bf16)


def x_before(rows):
    return jnp.where(lane_of(rows.shape) % HALF == 0, 0.0, pltpu.roll(rows, 1, 1))


def x_after(rows):
    return jnp.where(lane_of(rows.shape) % HALF == HALF - 1, 0.0, pltpu.roll(rows, LANES - 1, 1))


def at(group):
    return slice(group * LANES, (group + 1) * LANES)


def arrange_body(vol, a0, row, plane, corner, rows):
    for z in range(8):
        tops = [c * 128 + z * 16 + yb * 8 for yb in range(2) for c in range(4)]
        cube = jnp.stack([vol[top : top + 8, :] for top in tops], axis=0)
        rows[z * 64 : z * 64 + 64, :] = jnp.transpose(cube, (1, 0, 2)).reshape(64, 512)
    x_at = lax.broadcasted_iota(jnp.int32, (512, 512), 0)
    to = lax.broadcasted_iota(jnp.int32, (512, 512), 1)
    move = jnp.where(x_at == (to % HALF) * 8 + to // HALF, 1.0, 0.0).astype(bf16)
    phased = dot(rows[...].astype(bf16), move)
    parts = []
    for j in range(4):
        part = phased[:, at(j)].reshape(64, 8, LANES)
        turned = pltpu.roll(pltpu.roll(part, 4, 1), HALF, 2)
        sub = lax.broadcasted_iota(jnp.int32, part.shape, 1)
        parts.append(jnp.where((sub < 4) == (lane_of(part.shape) < HALF), part, turned))
    whole = jnp.concatenate(parts, axis=1).astype(bf16)
    a0[...] = whole.reshape(8, 8, 32, LANES)
    plane[...] = a0[1:]
    for z in range(8):
        for yp in range(1, 8):
            half = upper_half(a0[z, yp])
            row[z, 16 * yp - 16 : 16 * yp, :] = half
            if z > 0:
                corner[z - 1, 16 * yp - 16 : 16 * yp, :] = half


def weights_body(w1, w2, w3, t1, t2, t3, tt2, tt3):
    eye = jnp.where(
        lax.broadcasted_iota(jnp.int32, (HALF, LANES), 0) == lane_of((HALF, LANES)), 1.0, 0.0
    ).astype(bf16)
    blocks = []
    for ab in range(9):
        both, low = w1[ab, 0], w1[ab, 1]
        for m in range(4):
            block = pltpu.roll(both, 16 * m, 1) if m else both
            if m < 3:
                block = block + pltpu.roll(low, 16 * (m + 1), 1)
            blocks.append(block)
        blocks += [jnp.zeros_like(low), low]
    t1[...] = dot_nt(eye, jnp.concatenate(blocks, axis=0).astype(bf16)).astype(bf16)
    blocks = []
    for ab in range(9):
        e0, e1, e2 = w2[3 * ab], w2[3 * ab + 1], w2[3 * ab + 2]
        blocks += [e1, e2 + pltpu.roll(e0, 32, 1), pltpu.roll(e1, 32, 1), pltpu.roll(e2, 32, 1), e0]
    tt2[...] = jnp.concatenate(blocks, axis=0).astype(bf16)
    t2[...] = dot_nt(eye, tt2[...]).astype(bf16)
    blocks = []
    for ab in range(9):
        blocks += [w3[3 * ab + 1], w3[3 * ab + 2], w3[3 * ab]]
    tt3[...] = jnp.concatenate(blocks, axis=0).astype(bf16)
    t3[...] = dot_nt(eye, tt3[...]).astype(bf16)


def fill_patches(tile, low, high, rows, moved, out):
    step, count = rows + moved, high - low + 1
    for zz in range(2 * low - 1, 2 * high + 2):
        for yy in range(2 * low - 1, 2 * high + 2):
            cell = tile(zz, yy)
            shifted = x_before(cell[rows - moved :].astype(f32)).astype(bf16)
            for a in range(3):
                for b in range(3):
                    i, j = zz + 1 - a, yy + 1 - b
                    if i % 2 or j % 2:
                        continue
                    i, j = i // 2 - low, j // 2 - low
                    if not (0 <= i < count and 0 <= j < count):
                        continue
                    top = (a * 3 + b) * step
                    out[top : top + rows, at(i * count + j)] = cell
                    out[top + rows : top + step, at(i * count + j)] = shifted


def finish(pre):
    root = jnp.sqrt(pre * pre + 1.0)
    return 0.65 * pre + 0.35 * (root - 1.0), 0.65 + 0.35 * pre / root


def forward_body(a0, row, plane, corner, t1, t2, t3, tt2, tt3, head, targets,
                 p1, kept, slopes, sums, a1, a2):
    def tile_one(zz, yy):
        own = a0[zz, yy % 8] if zz >= 0 else plane[zz + 7, yy % 8]
        if yy >= 0:
            return own
        part = slice(16 * (yy + 7), 16 * (yy + 8))
        return row_below(own, row[zz, part, :] if zz >= 0 else corner[zz + 7, part, :])

    fill_patches(tile_one, -3, 3, 32, 16, p1)
    act, slopes[:, : 49 * LANES] = finish(dot(t1[...], p1[...]))
    a1[...] = act.astype(bf16)
    fill_patches(lambda z, y: a1[:, at((z + 3) * 7 + y + 3)], -1, 1, 64, 16, kept)
    act, slopes[:, AT_TWO : AT_TWO + 9 * LANES] = finish(dot(t2[...], kept[:720, : 9 * LANES]))
    a2[...] = act.astype(bf16)
    fill_patches(lambda z, y: a2[:, at((z + 1) * 3 + y + 1)], 0, 0, 64, 32, kept.at[:, at(9)])
    act, slopes[:, at(58)] = finish(dot(t3[...], kept[:, at(9)]))
    column = jnp.sum(act.astype(bf16).astype(f32), axis=1, keepdims=True)
    spot = lax.broadcasted_iota(jnp.int32, (HALF, LANES), 0) == lane_of((HALF, LANES))
    line = jnp.sum(jnp.where(spot, column, 0.0), axis=0, keepdims=True)
    sums[...] = jnp.broadcast_to(line, sums.shape)
    kept[:720, at(10)] = tt2[...]
    kept[:, at(11)] = tt3[...]
    slopes[:4, AT_HEAD : AT_HEAD + HALF] = head[...]
    spot = lax.broadcasted_iota(jnp.int32, (4, 4), 0) == lane_of((4, 4))
    column = jnp.sum(jnp.where(spot, targets[...], 0.0), axis=1, keepdims=True)
    slopes[8:12, AT_HEAD : AT_HEAD + LANES] = jnp.broadcast_to(column, (4, LANES))


def reach(index):
    return [(1, index // 2)] if index % 2 == 0 else [(2, index // 2), (0, index // 2 + 1)]


def back_cell(terms, z, y, step, rows, low, high):
    total = None
    for a, i in reach(z):
        for b, j in reach(y):
            if low <= i <= high and low <= j <= high:
                top = (a * 3 + b) * step
                part = terms[top : top + step, at((i - low) * (high - low + 1) + j - low)]
                total = part if total is None else total + part
    moved = step - rows
    last = total[rows - moved : rows] + x_after(total[rows:])
    return jnp.concatenate([total[: rows - moved], last], axis=0)


def backward_body(cells, share, gathered, p1, kept, slopes,
                  result, out, err3, err2, err1, terms3, terms2):
    head = slopes[:4, AT_HEAD : AT_HEAD + HALF]
    targets = slopes[8:12, AT_HEAD : AT_HEAD + 1]
    out[...] = jnp.zeros_like(out)
    pooled = jnp.sum(gathered[...], axis=0, keepdims=True)[:, :HALF] / cells
    errors = jnp.sum(head * pooled, axis=1, keepdims=True) - targets
    outer = errors * pooled * share
    loss = 0.5 * jnp.sum(errors * errors, axis=0, keepdims=True) * share
    exact = [jnp.concatenate([outer[0:1], outer[1:2]], axis=1),
             jnp.concatenate([outer[2:3], outer[3:4]], axis=1),
             jnp.broadcast_to(loss, (1, LANES))]
    for k, value in enumerate(exact):
        first = value.astype(bf16).astype(f32)
        out[k, HIGH : HIGH + 1, :] = first
        out[k, LOW : LOW + 1, :] = value - first
    line = jnp.sum(errors * head, axis=0, keepdims=True) / cells
    spot = lax.broadcasted_iota(jnp.int32, (HALF, HALF), 0) == lane_of((HALF, HALF))
    back_pool = jnp.sum(jnp.where(spot, line, 0.0), axis=1, keepdims=True)

    err3[:HALF, :] = (back_pool * slopes[:, at(58)]).astype(bf16)
    err3[HALF:, :] = jnp.zeros((HALF, LANES), bf16)
    err2[HALF:, :] = jnp.zeros((HALF, 9 * LANES), bf16)
    err1[HALF:, :] = jnp.zeros((HALF, 49 * LANES), bf16)
    terms3[...] = dot(kept[:, at(11)], err3[...])
    for k in range(9):
        back = back_cell(terms3, k // 3 - 1, k % 3 - 1, 96, 64, 0, 0)
        err2[:HALF, at(k)] = (back * slopes[:, at(49 + k)]).astype(bf16)
    terms2[...] = dot(kept[:720, at(10)], err2[...])
    for k in range(49):
        back = back_cell(terms2, k // 7 - 3, k % 7 - 3, 80, 64, -1, 1)
        err1[:HALF, at(k)] = (back * slopes[:, at(k)]).astype(bf16)

    grad = dot_nt(kept[:, at(9)], err3[...])
    taps = [96 * ab + 32 * ((e + 2) % 3) for ab in range(9) for e in range(3)]
    for k, top in enumerate(taps[:14]):
        block = grad[top : top + 32]
        if k + 14 < 27:
            other = taps[k + 14]
            block = block + pltpu.roll(grad[other : other + 32], HALF, 1)
        out[k, :32, :] = block

    grad = dot_nt(kept[:720, : 9 * LANES], err2[...])
    blocks = []
    for ab in range(9):
        x = [grad[80 * ab + 16 * i : 80 * ab + 16 * i + 16] for i in range(5)]
        for first, second in ((4, 1), (0, 2), (1, 3)):
            block = x[first] + pltpu.roll(x[second], LANES - 32, 1)
            blocks.append(jnp.where(lane_of(block.shape) < 32, block, 0.0))
    for k in range(7):
        block = blocks[k]
        for m in range(1, 4):
            if k + 7 * m < 27:
                block = block + pltpu.roll(blocks[k + 7 * m], 32 * m, 1)
        for i, (chunk, top) in enumerate(places_two(k)):
            out[chunk, top : top + 8, :] = block[8 * i : 8 * i + 8]

    grad = dot_nt(p1[...], err1[...])
    blocks = []
    for ab in range(9):
        x = [grad[48 * ab + 8 * i : 48 * ab + 8 * i + 8] for i in range(6)]
        both, low = x[0], x[5]
        for m in range(1, 4):
            both = both + pltpu.roll(x[m], LANES - 16 * m, 1)
            low = low + pltpu.roll(x[m - 1], LANES - 16 * m, 1)
        low = jnp.where(lax.broadcasted_iota(jnp.int32, low.shape, 0) >= 4, low, 0.0)
        block = jnp.concatenate([both, low], axis=0)
        blocks.append(jnp.where(lane_of(block.shape) < 16, block, 0.0))
    block = blocks[0]
    for m in range(1, 8):
        block = block + pltpu.roll(blocks[m], 16 * m, 1)
    for m, block in enumerate((block, blocks[8])):
        for i, (chunk, top) in enumerate(places_one(m)):
            out[chunk, top : top + 8, :] = block[8 * i : 8 * i + 8]
    result[...] = out[...].astype(bf16)


def places_two(k):
    if k < 4:
        return [(14 + k // 2, 16 * (k % 2)), (14 + k // 2, 16 * (k % 2) + 8)]
    return [(2 * k - 8, 32), (2 * k - 7, 32)]


def places_one(m):
    return [(6 + 2 * m, 32), (7 + 2 * m, 32)]


def total_body(parts, out):
    total = parts[0].astype(f32)
    for k in range(1, parts.shape[0]):
        total = total + parts[k].astype(f32)
    exact = total[HIGH : HIGH + 1] + total[LOW : LOW + 1]
    first = exact.astype(bf16).astype(f32)
    at_row = lax.broadcasted_iota(jnp.int32, total.shape, 0)
    total = jnp.where(at_row == HIGH, first, jnp.where(at_row == LOW, exact - first, total))
    total = total.astype(bf16)
    for k in range(out.shape[0]):
        out[k] = total


def update_body(sent, u1, u2, u3, uh, loss, total):
    total[...] = sent[...].astype(f32)

    def scale(blocks, count):
        mean = 0.0
        for block in blocks:
            squares = jnp.sum(block * block, axis=0, keepdims=True)
            mean = mean + jnp.sum(squares, axis=1, keepdims=True) / count
        return 1.0 / jnp.sqrt(mean + epsilon)

    def read(places):
        return jnp.concatenate([total[chunk, top : top + 8, :] for chunk, top in places], axis=0)

    blocks = [total[k, :32, :] for k in range(14)]
    factor = scale(blocks, 64 * 32 * 27)
    for k, block in enumerate(blocks):
        block = block * factor
        u3[k] = block[:, :HALF]
        if k + 14 < 27:
            u3[k + 14] = pltpu.roll(block, HALF, 1)[:, :HALF]
    blocks = [read(places_two(k)) for k in range(7)]
    factor = scale(blocks, 32 * 16 * 27)
    for k, block in enumerate(blocks):
        block = block * factor
        for m in range(4):
            if k + 7 * m < 27:
                u2[k + 7 * m] = (pltpu.roll(block, LANES - 32 * m, 1) if m else block)[:, :32]
    blocks = [read(places_one(m)) for m in range(2)]
    factor = scale(blocks, 16 * 4 * 27)
    for ab in range(9):
        m = ab % 8
        block = blocks[ab // 8] * factor
        block = (pltpu.roll(block, LANES - 16 * m, 1) if m else block)[:, :16]
        u1[3 * ab] = block[12:16]
        u1[3 * ab + 1] = block[0:4]
        u1[3 * ab + 2] = block[4:8]
    exact = [total[k, HIGH : HIGH + 1, :] + total[k, LOW : LOW + 1, :] for k in range(3)]
    factor = scale(exact[:2], 4 * 64)
    for k in range(2):
        line = exact[k] * factor
        uh[2 * k : 2 * k + 1, :] = line[:, :HALF]
        uh[2 * k + 1 : 2 * k + 2, :] = pltpu.roll(line, HALF, 1)[:, :HALF]
    loss[...] = exact[2]


def neighbours(by):
    gz, gy = lax.axis_size("gz"), lax.axis_size("gy")
    z = [(i, i + by) for i in range(gz) if 0 <= i + by < gz]
    y = [(i, i + by) for i in range(gy) if 0 <= i + by < gy]
    corner = [(i * gy + j, k * gy + l) for i, k in z for j, l in y]
    return y, z, corner


def exchange(row, plane, corner, by):
    y, z, both = neighbours(by)
    plane = lax.ppermute(plane, "gz", z)
    corner = lax.ppermute(corner, ("gz", "gy"), both)
    return lax.ppermute(row, "gy", y), plane, corner


def summed_over_all(parts):
    beyond = lax.axis_size(("batch", "gz"))
    parts = lax.all_to_all(parts, "gy", 0, 0, tiled=True)
    (parts,) = call(total_body, [((beyond, ROWS, LANES), bf16)], (parts,))
    parts = lax.all_to_all(parts, ("batch", "gz"), 0, 0, tiled=True)
    (parts,) = call(total_body, [((CHUNKS, ROWS, LANES), bf16)], (parts,))
    return lax.all_to_all(parts, "gy", 0, 0, tiled=True)


def local(volume, conv_one, conv_two, conv_three, head_weight, targets):
    devices = lax.axis_size("gz") * lax.axis_size("gy")
    cells = float(devices * LANES)

    def taps(w):
        w = jnp.transpose(w, (2, 3, 4, 1, 0)).astype(f32)
        return jnp.pad(w.reshape((27,) + w.shape[3:]), ((0, 0), (0, 0), (0, LANES - w.shape[4])))

    w1 = taps(conv_one).reshape(9, 3, 4, LANES)
    both = w1[:, 1:].reshape(9, 1, 8, LANES)
    low = jnp.pad(w1[:, :1], ((0, 0), (0, 0), (4, 0), (0, 0)))
    t1, t2, t3, tt2, tt3 = call(
        weights_body,
        [((64, 432), bf16), ((64, 720), bf16), ((64, 864), bf16), ((720, LANES), bf16), ((864, LANES), bf16)],
        (jnp.concatenate([both, low], axis=1), taps(conv_two), taps(conv_three)),
    )
    a0, row, plane, corner = call(
        arrange_body,
        [((8, 8, 32, LANES), bf16), ((8, 112, LANES), bf16), ((7, 8, 32, LANES), bf16), ((7, 112, LANES), bf16)],
        (volume.reshape(512, 512),),
        [((512, 512), f32)],
    )
    row, plane, corner = exchange(row, plane, corner, 1)
    p1, kept, slopes, sums = call(
        forward_body,
        [((432, 49 * LANES), bf16), ((864, 12 * LANES), bf16), ((64, 60 * LANES), f32), ((devices, LANES), f32)],
        (a0, row, plane, corner, t1, t2, t3, tt2, tt3, head_weight, targets),
        [((64, 49 * LANES), bf16), ((64, 9 * LANES), bf16)],
        24,
    )
    pooled = lax.all_to_all(sums, ("gz", "gy"), 0, 0, tiled=True)
    (flat,) = call(
        functools.partial(backward_body, cells, 1.0 / devices),
        [((CHUNKS, ROWS, LANES), bf16)],
        (pooled, p1, kept, slopes),
        [((CHUNKS, ROWS, LANES), f32), ((LANES, LANES), bf16), ((LANES, 9 * LANES), bf16),
         ((LANES, 49 * LANES), bf16), ((864, LANES), f32), ((720, 9 * LANES), f32)],
        24,
    )
    u1, u2, u3, uh, loss = call(
        update_body,
        [((27, 4, 16), f32), ((27, 16, 32), f32), ((27, 32, 64), f32), ((4, 64), f32), ((1, LANES), f32)],
        (summed_over_all(flat),),
        [((CHUNKS, ROWS, LANES), f32)],
    )

    def kernel_form(u):
        return jnp.transpose(u.reshape((3, 3, 3) + u.shape[1:]), (4, 3, 0, 1, 2))

    return kernel_form(u1), kernel_form(u2), kernel_form(u3), uh, loss[0, 0]


def solution(mesh):
    in_specs = (P("batch", None, "gz", "gy", None), P(), P(), P(), P(), P("batch", None))
    out_specs = (P(), P(), P(), P(), P())
    return jax.shard_map(local, mesh=mesh, in_specs=in_specs, out_specs=out_specs, check_vma=False)
```

```python
import functools
import jax
import jax.numpy as jnp
from jax import lax
from jax.experimental import pallas as pl
from jax.experimental.pallas import tpu as pltpu
from jax.sharding import PartitionSpec as P

epsilon = 1e-06
f32 = jnp.float32
bf16 = jnp.bfloat16
LANES = 128
HALF = 64
CHUNKS, ROWS = 16, 40
EXACT, HIGH, LOW = 10, 32, 35
AT_TWO, AT_THREE, AT_HEAD = 49, 58, 59 * LANES


def call(body, outs, args, scratch=(), mib=8, spaces=None):
    return pl.pallas_call(
        body,
        out_shape=[jax.ShapeDtypeStruct(s, d) for s, d in outs],
        in_specs=[pl.BlockSpec(memory_space=m) for m in spaces or [pltpu.VMEM] * len(args)],
        out_specs=[pl.BlockSpec(memory_space=pltpu.VMEM)] * len(outs),
        scratch_shapes=[pltpu.VMEM(*s) if isinstance(s, tuple) else s for s in scratch],
        compiler_params=pltpu.CompilerParams(vmem_limit_bytes=mib * 1024 * 1024),
    )(*args)


def lane_of(shape):
    return lax.broadcasted_iota(jnp.int32, shape, len(shape) - 1)


def dot(a, b):
    return lax.dot_general(a, b, (((1,), (0,)), ((), ())), preferred_element_type=f32)


def dot_nt(a, b):
    return lax.dot_general(a, b, (((1,), (1,)), ((), ())), preferred_element_type=f32)


def upper_half(tile):
    top, bottom = tile[:16].astype(f32), tile[16:].astype(f32)
    return jnp.where(lane_of(top.shape) < HALF, pltpu.roll(top, HALF, 1), bottom).astype(bf16)


def lower_half(tile):
    top, bottom = tile[:16].astype(f32), tile[16:].astype(f32)
    return jnp.where(lane_of(top.shape) < HALF, top, pltpu.roll(bottom, HALF, 1)).astype(bf16)


def joined(received, inside, upper):
    got = received.astype(f32) * inside
    low = lane_of(got.shape) < HALF
    top = jnp.where(low, got, upper[:16])
    bottom = jnp.where(low, pltpu.roll(got, HALF, 1), upper[16:])
    return jnp.concatenate([top, bottom], axis=0).astype(bf16)


def x_before(rows):
    return jnp.where(lane_of(rows.shape) % HALF == 0, 0.0, pltpu.roll(rows, 1, 1))


def x_after(rows):
    return jnp.where(lane_of(rows.shape) % HALF == HALF - 1, 0.0, pltpu.roll(rows, LANES - 1, 1))


def at(group):
    return slice(group * LANES, (group + 1) * LANES)


def arrange_body(vol, a0, row, below, corner, rows):
    for z in range(8):
        tops = [c * 128 + z * 16 + yb * 8 for yb in range(2) for c in range(4)]
        cube = jnp.stack([vol[top : top + 8, :] for top in tops], axis=0)
        rows[z * 64 : z * 64 + 64, :] = jnp.transpose(cube, (1, 0, 2)).reshape(64, 512)
    x_at = lax.broadcasted_iota(jnp.int32, (512, 512), 0)
    to = lax.broadcasted_iota(jnp.int32, (512, 512), 1)
    move = jnp.where(x_at == (to % HALF) * 8 + to // HALF, 1.0, 0.0).astype(bf16)
    phased = dot(rows[...].astype(bf16), move)
    parts = []
    for j in range(4):
        part = phased[:, at(j)].reshape(64, 8, LANES)
        turned = pltpu.roll(pltpu.roll(part, 4, 1), HALF, 2)
        sub = lax.broadcasted_iota(jnp.int32, part.shape, 1)
        parts.append(jnp.where((sub < 4) == (lane_of(part.shape) < HALF), part, turned))
    whole = jnp.concatenate(parts, axis=1).astype(bf16)
    a0[...] = whole.reshape(8, 8, 32, LANES)
    for z in range(8):
        for yp in range(8):
            if z > 0:
                below[z - 1, 16 * yp : 16 * yp + 16, :] = lower_half(a0[z, yp])
        for yp in range(1, 8):
            half = upper_half(a0[z, yp])
            row[z, 16 * yp - 16 : 16 * yp, :] = half
            if z > 0:
                corner[z - 1, 16 * yp - 16 : 16 * yp, :] = half


def weights_body(w1, w2, w3, t1, t2, t3, tt2, tt3):
    eye = jnp.where(
        lax.broadcasted_iota(jnp.int32, (HALF, LANES), 0) == lane_of((HALF, LANES)), 1.0, 0.0
    ).astype(bf16)
    blocks = []
    for ab in range(9):
        both, low = w1[ab, 0], w1[ab, 1]
        for m in range(4):
            block = pltpu.roll(both, 16 * m, 1) if m else both
            if m < 3:
                block = block + pltpu.roll(low, 16 * (m + 1), 1)
            blocks.append(block)
        blocks += [jnp.zeros_like(low), low]
    t1[...] = dot_nt(eye, jnp.concatenate(blocks, axis=0).astype(bf16)).astype(bf16)
    blocks = []
    for ab in range(9):
        e0, e1, e2 = w2[3 * ab], w2[3 * ab + 1], w2[3 * ab + 2]
        blocks += [e1, e2 + pltpu.roll(e0, 32, 1), pltpu.roll(e1, 32, 1), pltpu.roll(e2, 32, 1), e0]
    tt2[...] = jnp.concatenate(blocks, axis=0).astype(bf16)
    t2[...] = dot_nt(eye, tt2[...]).astype(bf16)
    blocks = []
    for ab in range(9):
        blocks += [w3[3 * ab + 1], w3[3 * ab + 2], w3[3 * ab]]
    tt3[...] = jnp.concatenate(blocks, axis=0).astype(bf16)
    t3[...] = dot_nt(eye, tt3[...]).astype(bf16)


def fill_patches(tile, z_range, y_range, rows, moved, out):
    (z_low, z_high), (y_low, y_high) = z_range, y_range
    step, deep, wide = rows + moved, z_high - z_low + 1, y_high - y_low + 1
    for zz in range(2 * z_low - 1, 2 * z_high + 2):
        for yy in range(2 * y_low - 1, 2 * y_high + 2):
            cell = tile(zz, yy)
            shifted = x_before(cell[rows - moved :].astype(f32)).astype(bf16)
            for a in range(3):
                for b in range(3):
                    i, j = zz + 1 - a, yy + 1 - b
                    if i % 2 or j % 2:
                        continue
                    i, j = i // 2 - z_low, j // 2 - y_low
                    if not (0 <= i < deep and 0 <= j < wide):
                        continue
                    top = (a * 3 + b) * step
                    out[top : top + rows, at(i * wide + j)] = cell
                    out[top + rows : top + step, at(i * wide + j)] = shifted


def finish(pre):
    root = jnp.sqrt(pre * pre + 1.0)
    return 0.65 * pre + 0.35 * (root - 1.0), 0.65 + 0.35 * pre / root


def forward_body(a0, above, row, below, corner, t1, t2, t3, tt2, tt3, head, targets, inside,
                 p1, kept, slopes, sums, a1, a2):
    in_upper = jnp.full((32, LANES), inside[0], f32)
    in_row = jnp.full((16, LANES), inside[1], f32)
    in_below = jnp.full((16, LANES), inside[2], f32)
    in_corner = in_row * in_below

    def tile_one(zz, yy):
        yp = yy % 8
        part = slice(16 * (yy + 7), 16 * (yy + 8))
        if zz >= 0:
            upper = above[zz, yp].astype(f32)
            if yy < 0:
                return joined(row[zz, part, :], in_row, pltpu.roll(upper, HALF, 1))
            own = a0[zz, yp].astype(f32)
            return jnp.where(lane_of(own.shape) < HALF, own, upper).astype(bf16)
        upper = a0[zz + 8, yp].astype(f32) * in_upper
        if yy < 0:
            return joined(corner[zz + 7, part, :], in_corner, pltpu.roll(upper, HALF, 1))
        return joined(below[zz + 7, 16 * yp : 16 * yp + 16, :], in_below, upper)

    fill_patches(tile_one, (-3, 3), (-3, 3), 32, 16, p1)
    act, slopes[:, : 49 * LANES] = finish(dot(t1[...], p1[...]))
    a1[...] = act.astype(bf16)
    fill_patches(lambda z, y: a1[:, at((z + 3) * 7 + y + 3)], (-1, 1), (-1, 1), 64, 16, kept)
    act, slopes[:, AT_TWO * LANES : AT_THREE * LANES] = finish(dot(t2[...], kept[:720, : 9 * LANES]))
    a2[...] = act.astype(bf16)
    fill_patches(lambda z, y: a2[:, at((z + 1) * 3 + y + 1)], (0, 0), (0, 0), 64, 32, kept.at[:, at(9)])
    act, slopes[:, at(AT_THREE)] = finish(dot(t3[...], kept[:, at(9)]))
    column = jnp.sum(act.astype(bf16).astype(f32), axis=1, keepdims=True)
    spot = lax.broadcasted_iota(jnp.int32, (HALF, LANES), 0) == lane_of((HALF, LANES))
    line = jnp.sum(jnp.where(spot, column, 0.0), axis=0, keepdims=True)
    sums[...] = jnp.broadcast_to(line, sums.shape)
    kept[:720, at(10)] = tt2[...]
    kept[:, at(11)] = tt3[...]
    slopes[:4, AT_HEAD : AT_HEAD + HALF] = head[...]
    spot = lax.broadcasted_iota(jnp.int32, (4, 4), 0) == lane_of((4, 4))
    column = jnp.sum(jnp.where(spot, targets[...], 0.0), axis=1, keepdims=True)
    slopes[8:12, AT_HEAD : AT_HEAD + LANES] = jnp.broadcast_to(column, (4, LANES))


def reach(index):
    return [(1, index // 2)] if index % 2 == 0 else [(2, index // 2), (0, index // 2 + 1)]


def back_cell(terms, z, y, step, rows, low, high):
    total = None
    for a, i in reach(z):
        for b, j in reach(y):
            if low <= i <= high and low <= j <= high:
                top = (a * 3 + b) * step
                part = terms[top : top + step, at((i - low) * (high - low + 1) + j - low)]
                total = part if total is None else total + part
    moved = step - rows
    last = total[rows - moved : rows] + x_after(total[rows:])
    return jnp.concatenate([total[: rows - moved], last], axis=0)


def backward_body(cells, share, gathered, p1, kept, slopes,
                  result, out, err3, err2, err1, terms3, terms2):
    head = slopes[:4, AT_HEAD : AT_HEAD + HALF]
    targets = slopes[8:12, AT_HEAD : AT_HEAD + 1]
    out[...] = jnp.zeros_like(out)
    pooled = jnp.sum(gathered[...], axis=0, keepdims=True)[:, :HALF] / cells
    errors = jnp.sum(head * pooled, axis=1, keepdims=True) - targets
    outer = errors * pooled * share
    loss = 0.5 * jnp.sum(errors * errors, axis=0, keepdims=True) * share
    exact = [jnp.concatenate([outer[0:1], outer[1:2]], axis=1),
             jnp.concatenate([outer[2:3], outer[3:4]], axis=1),
             jnp.broadcast_to(loss, (1, LANES))]
    for k, value in enumerate(exact):
        first = value.astype(bf16).astype(f32)
        out[EXACT, HIGH + k : HIGH + k + 1, :] = first
        out[EXACT, LOW + k : LOW + k + 1, :] = value - first
    line = jnp.sum(errors * head, axis=0, keepdims=True) / cells
    spot = lax.broadcasted_iota(jnp.int32, (HALF, HALF), 0) == lane_of((HALF, HALF))
    back_pool = jnp.sum(jnp.where(spot, line, 0.0), axis=1, keepdims=True)

    err3[:HALF, :] = (back_pool * slopes[:, at(AT_THREE)]).astype(bf16)
    err3[HALF:, :] = jnp.zeros((HALF, LANES), bf16)
    err2[HALF:, :] = jnp.zeros((HALF, 9 * LANES), bf16)
    err1[HALF:, :] = jnp.zeros((HALF, 49 * LANES), bf16)
    terms3[...] = dot(kept[:, at(11)], err3[...])
    for k in range(9):
        back = back_cell(terms3, k // 3 - 1, k % 3 - 1, 96, 64, 0, 0)
        err2[:HALF, at(k)] = (back * slopes[:, at(AT_TWO + k)]).astype(bf16)
    terms2[...] = dot(kept[:720, at(10)], err2[...])
    for k in range(49):
        back = back_cell(terms2, k // 7 - 3, k % 7 - 3, 80, 64, -1, 1)
        err1[:HALF, at(k)] = (back * slopes[:, at(k)]).astype(bf16)

    grad = dot_nt(kept[:, at(9)], err3[...])
    taps = [96 * ab + 32 * ((e + 2) % 3) for ab in range(9) for e in range(3)]
    for k, top in enumerate(taps[:14]):
        block = grad[top : top + 32]
        if k + 14 < 27:
            other = taps[k + 14]
            block = block + pltpu.roll(grad[other : other + 32], HALF, 1)
        out[k, :32, :] = block

    grad = dot_nt(kept[:720, : 9 * LANES], err2[...])
    blocks = []
    for ab in range(9):
        x = [grad[80 * ab + 16 * i : 80 * ab + 16 * i + 16] for i in range(5)]
        for first, second in ((4, 1), (0, 2), (1, 3)):
            block = x[first] + pltpu.roll(x[second], LANES - 32, 1)
            blocks.append(jnp.where(lane_of(block.shape) < 32, block, 0.0))
    for k in range(7):
        block = blocks[k]
        for m in range(1, 4):
            if k + 7 * m < 27:
                block = block + pltpu.roll(blocks[k + 7 * m], 32 * m, 1)
        for i, (chunk, top) in enumerate(places_two(k)):
            out[chunk, top : top + 8, :] = block[8 * i : 8 * i + 8]

    grad = dot_nt(p1[...], err1[...])
    blocks = []
    for ab in range(9):
        x = [grad[48 * ab + 8 * i : 48 * ab + 8 * i + 8] for i in range(6)]
        both, low = x[0], x[5]
        for m in range(1, 4):
            both = both + pltpu.roll(x[m], LANES - 16 * m, 1)
            low = low + pltpu.roll(x[m - 1], LANES - 16 * m, 1)
        low = jnp.where(lax.broadcasted_iota(jnp.int32, low.shape, 0) >= 4, low, 0.0)
        block = jnp.concatenate([both, low], axis=0)
        blocks.append(jnp.where(lane_of(block.shape) < 16, block, 0.0))
    block = blocks[0]
    for m in range(1, 8):
        block = block + pltpu.roll(blocks[m], 16 * m, 1)
    for m, block in enumerate((block, blocks[8])):
        for i, (chunk, top) in enumerate(places_one(m)):
            out[chunk, top : top + 8, :] = block[8 * i : 8 * i + 8]
    result[...] = out[...].astype(bf16)


def places_two(k):
    if k < 4:
        return [(14 + k // 2, 16 * (k % 2)), (14 + k // 2, 16 * (k % 2) + 8)]
    return [(2 * k - 8, 32), (2 * k - 7, 32)]


def places_one(m):
    return [(6 + 2 * m, 32), (7 + 2 * m, 32)]


def total_body(parts, chunk, out):
    total = parts[0].astype(f32)
    for k in range(1, parts.shape[0]):
        total = total + parts[k].astype(f32)
    exact = total[HIGH:LOW] + total[LOW : LOW + 3]
    first = exact.astype(bf16).astype(f32)
    tail = jnp.concatenate([first, exact - first, total[LOW + 3 :]], axis=0)
    tail = jnp.where(chunk[0] == EXACT, tail, total[HIGH:])
    total = jnp.concatenate([total[:HIGH], tail], axis=0).astype(bf16)
    for k in range(out.shape[0]):
        out[k] = total


def update_body(sent, u1, u2, u3, uh, loss, total):
    total[...] = sent[...].astype(f32)

    def scale(blocks, count):
        mean = 0.0
        for block in blocks:
            squares = jnp.sum(block * block, axis=0, keepdims=True)
            mean = mean + jnp.sum(squares, axis=1, keepdims=True) / count
        return 1.0 / jnp.sqrt(mean + epsilon)

    def read(places):
        return jnp.concatenate([total[chunk, top : top + 8, :] for chunk, top in places], axis=0)

    blocks = [total[k, :32, :] for k in range(14)]
    factor = scale(blocks, 64 * 32 * 27)
    for k, block in enumerate(blocks):
        block = block * factor
        u3[k] = block[:, :HALF]
        if k + 14 < 27:
            u3[k + 14] = pltpu.roll(block, HALF, 1)[:, :HALF]
    blocks = [read(places_two(k)) for k in range(7)]
    factor = scale(blocks, 32 * 16 * 27)
    for k, block in enumerate(blocks):
        block = block * factor
        for m in range(4):
            if k + 7 * m < 27:
                u2[k + 7 * m] = (pltpu.roll(block, LANES - 32 * m, 1) if m else block)[:, :32]
    blocks = [read(places_one(m)) for m in range(2)]
    factor = scale(blocks, 16 * 4 * 27)
    for ab in range(9):
        m = ab % 8
        block = blocks[ab // 8] * factor
        block = (pltpu.roll(block, LANES - 16 * m, 1) if m else block)[:, :16]
        u1[3 * ab] = block[12:16]
        u1[3 * ab + 1] = block[0:4]
        u1[3 * ab + 2] = block[4:8]
    exact = [total[EXACT, HIGH + k : HIGH + k + 1, :] + total[EXACT, LOW + k : LOW + k + 1, :]
             for k in range(3)]
    factor = scale(exact[:2], 4 * 64)
    for k in range(2):
        line = exact[k] * factor
        uh[2 * k : 2 * k + 1, :] = line[:, :HALF]
        uh[2 * k + 1 : 2 * k + 2, :] = pltpu.roll(line, HALF, 1)[:, :HALF]
    loss[...] = exact[2]


def exchange(whole, row, below, corner):
    gz, gy = lax.axis_size("gz"), lax.axis_size("gy")
    z, y = [(i, (i + 1) % gz) for i in range(gz)], [(i, (i + 1) % gy) for i in range(gy)]
    both = [(i * gy + j, k * gy + l) for i, k in z for j, l in y]
    above = lax.ppermute(whole, "gz", [(k, i) for i, k in z])
    below = lax.ppermute(below, "gz", z)
    corner = lax.ppermute(corner, ("gz", "gy"), both)
    return above, lax.ppermute(row, "gy", y), below, corner


def summed_over_all(parts, chunk):
    beyond = lax.axis_size(("batch", "gz"))
    spaces = (pltpu.VMEM, pltpu.SMEM)
    parts = lax.all_to_all(parts, "gy", 0, 0, tiled=True)
    (parts,) = call(total_body, [((beyond, ROWS, LANES), bf16)], (parts, chunk), spaces=spaces)
    parts = lax.all_to_all(parts, ("batch", "gz"), 0, 0, tiled=True)
    (parts,) = call(total_body, [((CHUNKS, ROWS, LANES), bf16)], (parts, chunk), spaces=spaces)
    return lax.all_to_all(parts, "gy", 0, 0, tiled=True)


def local(volume, conv_one, conv_two, conv_three, head_weight, targets):
    devices = lax.axis_size("gz") * lax.axis_size("gy")
    cells = float(devices * LANES)
    z_at, y_at = lax.axis_index("gz"), lax.axis_index("gy")
    inside = jnp.stack([z_at < lax.axis_size("gz") - 1, y_at > 0, z_at > 0]).astype(f32)
    chunk = y_at.astype(jnp.int32).reshape(1)
    volume, chunk, inside = lax.optimization_barrier((volume, chunk, inside))

    def taps(w):
        w = jnp.transpose(w, (2, 3, 4, 1, 0)).astype(f32)
        return jnp.pad(w.reshape((27,) + w.shape[3:]), ((0, 0), (0, 0), (0, LANES - w.shape[4])))

    w1 = taps(conv_one).reshape(9, 3, 4, LANES)
    both = w1[:, 1:].reshape(9, 1, 8, LANES)
    low = jnp.pad(w1[:, :1], ((0, 0), (0, 0), (4, 0), (0, 0)))
    t1, t2, t3, tt2, tt3 = call(
        weights_body,
        [((64, 432), bf16), ((64, 720), bf16), ((64, 864), bf16), ((720, LANES), bf16), ((864, LANES), bf16)],
        (jnp.concatenate([both, low], axis=1), taps(conv_two), taps(conv_three)),
    )
    a0, row, below, corner = call(
        arrange_body,
        [((8, 8, 32, LANES), bf16), ((8, 112, LANES), bf16), ((7, LANES, LANES), bf16), ((7, 112, LANES), bf16)],
        (volume.reshape(512, 512),),
        [((512, 512), f32)],
    )
    above, row, below, corner = exchange(a0, row, below, corner)
    p1, kept, slopes, sums = call(
        forward_body,
        [((432, 49 * LANES), bf16), ((864, 12 * LANES), bf16), ((64, 60 * LANES), f32), ((devices, LANES), f32)],
        (a0, above, row, below, corner, t1, t2, t3, tt2, tt3, head_weight, targets, inside),
        [((64, 49 * LANES), bf16), ((64, 9 * LANES), bf16)],
        24,
        [pltpu.VMEM] * 12 + [pltpu.SMEM],
    )
    pooled = lax.all_to_all(sums, ("gz", "gy"), 0, 0, tiled=True)
    (flat,) = call(
        functools.partial(backward_body, cells, 1.0 / devices),
        [((CHUNKS, ROWS, LANES), bf16)],
        (pooled, p1, kept, slopes),
        [((CHUNKS, ROWS, LANES), f32), ((LANES, LANES), bf16), ((LANES, 9 * LANES), bf16),
         ((LANES, 49 * LANES), bf16), ((864, LANES), f32), ((720, 9 * LANES), f32)],
        24,
    )
    u1, u2, u3, uh, loss = call(
        update_body,
        [((27, 4, 16), f32), ((27, 16, 32), f32), ((27, 32, 64), f32), ((4, 64), f32), ((1, LANES), f32)],
        (summed_over_all(flat, chunk),),
        [((CHUNKS, ROWS, LANES), f32)],
    )

    def kernel_form(u):
        return jnp.transpose(u.reshape((3, 3, 3) + u.shape[1:]), (4, 3, 0, 1, 2))

    return kernel_form(u1), kernel_form(u2), kernel_form(u3), uh, loss[0, 0]


def solution(mesh):
    in_specs = (P("batch", None, "gz", "gy", None), P(), P(), P(), P(), P("batch", None))
    out_specs = (P(), P(), P(), P(), P())
    return jax.shard_map(local, mesh=mesh, in_specs=in_specs, out_specs=out_specs, check_vma=False)
```

```python
import functools
import jax
import jax.numpy as jnp
from jax import lax
from jax.experimental import pallas as pl
from jax.experimental.pallas import tpu as pltpu
from jax.sharding import PartitionSpec as P

epsilon = 1e-06
f32 = jnp.float32
bf16 = jnp.bfloat16
LANES = 128
HALF = 64
CHUNKS, ROWS = 16, 40
EXACT, HIGH, LOW = 10, 32, 35
AT_TWO, AT_THREE, AT_HEAD = 49, 58, 59 * LANES


def call(body, outs, args, scratch=(), mib=8, spaces=None):
    return pl.pallas_call(
        body,
        out_shape=[jax.ShapeDtypeStruct(s, d) for s, d in outs],
        in_specs=[pl.BlockSpec(memory_space=m) for m in spaces or [pltpu.VMEM] * len(args)],
        out_specs=[pl.BlockSpec(memory_space=pltpu.VMEM)] * len(outs),
        scratch_shapes=[pltpu.VMEM(*s) if isinstance(s, tuple) else s for s in scratch],
        compiler_params=pltpu.CompilerParams(vmem_limit_bytes=mib * 1024 * 1024),
    )(*args)


def lane_of(shape):
    return lax.broadcasted_iota(jnp.int32, shape, len(shape) - 1)


def dot(a, b):
    return lax.dot_general(a, b, (((1,), (0,)), ((), ())), preferred_element_type=f32)


def dot_nt(a, b):
    return lax.dot_general(a, b, (((1,), (1,)), ((), ())), preferred_element_type=f32)


def upper_half(tile):
    top, bottom = tile[:16].astype(f32), tile[16:].astype(f32)
    return jnp.where(lane_of(top.shape) < HALF, pltpu.roll(top, HALF, 1), bottom).astype(bf16)


def lower_half(tile):
    top, bottom = tile[:16].astype(f32), tile[16:].astype(f32)
    return jnp.where(lane_of(top.shape) < HALF, top, pltpu.roll(bottom, HALF, 1)).astype(bf16)


def unpacked(received):
    turned = pltpu.roll(received.astype(f32), HALF, 1).astype(bf16)
    return jnp.concatenate([received, turned], axis=0)


def half_turned(tile):
    return pltpu.roll(tile.astype(f32), HALF, 1).astype(bf16)


def x_before(rows):
    return jnp.where(lane_of(rows.shape) % HALF == 0, 0.0, pltpu.roll(rows, 1, 1))


def x_after(rows):
    return jnp.where(lane_of(rows.shape) % HALF == HALF - 1, 0.0, pltpu.roll(rows, LANES - 1, 1))


def at(group):
    return slice(group * LANES, (group + 1) * LANES)


def arrange_body(vol, a0, row, below, corner, rows):
    for z in range(8):
        tops = [c * 128 + z * 16 + yb * 8 for yb in range(2) for c in range(4)]
        cube = jnp.stack([vol[top : top + 8, :] for top in tops], axis=0)
        rows[z * 64 : z * 64 + 64, :] = jnp.transpose(cube, (1, 0, 2)).reshape(64, 512)
    x_at = lax.broadcasted_iota(jnp.int32, (512, 512), 0)
    to = lax.broadcasted_iota(jnp.int32, (512, 512), 1)
    move = jnp.where(x_at == (to % HALF) * 8 + to // HALF, 1.0, 0.0).astype(bf16)
    phased = dot(rows[...].astype(bf16), move)
    parts = []
    for j in range(4):
        part = phased[:, at(j)].reshape(64, 8, LANES)
        turned = pltpu.roll(pltpu.roll(part, 4, 1), HALF, 2)
        sub = lax.broadcasted_iota(jnp.int32, part.shape, 1)
        parts.append(jnp.where((sub < 4) == (lane_of(part.shape) < HALF), part, turned))
    whole = jnp.concatenate(parts, axis=1).astype(bf16)
    a0[...] = whole.reshape(8, 8, 32, LANES)
    for z in range(8):
        for yp in range(8):
            if z > 0:
                below[z - 1, 16 * yp : 16 * yp + 16, :] = lower_half(a0[z, yp])
        for yp in range(1, 8):
            half = upper_half(a0[z, yp])
            row[z, 16 * yp - 16 : 16 * yp, :] = half
            if z > 0:
                corner[z - 1, 16 * yp - 16 : 16 * yp, :] = half


def weights_body(w1, w2, w3, t1, t2, t3, tt2, tt3):
    eye = jnp.where(
        lax.broadcasted_iota(jnp.int32, (HALF, LANES), 0) == lane_of((HALF, LANES)), 1.0, 0.0
    ).astype(bf16)
    blocks = []
    for ab in range(9):
        both, low = w1[ab, 0], w1[ab, 1]
        for m in range(4):
            block = pltpu.roll(both, 16 * m, 1) if m else both
            if m < 3:
                block = block + pltpu.roll(low, 16 * (m + 1), 1)
            blocks.append(block)
        blocks += [jnp.zeros_like(low), low]
    t1[...] = dot_nt(eye, jnp.concatenate(blocks, axis=0).astype(bf16)).astype(bf16)
    blocks = []
    for ab in range(9):
        e0, e1, e2 = w2[3 * ab], w2[3 * ab + 1], w2[3 * ab + 2]
        blocks += [e1, e2 + pltpu.roll(e0, 32, 1), pltpu.roll(e1, 32, 1), pltpu.roll(e2, 32, 1), e0]
    tt2[...] = jnp.concatenate(blocks, axis=0).astype(bf16)
    t2[...] = dot_nt(eye, tt2[...]).astype(bf16)
    blocks = []
    for ab in range(9):
        blocks += [w3[3 * ab + 1], w3[3 * ab + 2], w3[3 * ab]]
    tt3[...] = jnp.concatenate(blocks, axis=0).astype(bf16)
    t3[...] = dot_nt(eye, tt3[...]).astype(bf16)


def fill_patches(tile, z_range, y_range, rows, moved, out):
    (z_low, z_high), (y_low, y_high) = z_range, y_range
    step, deep, wide = rows + moved, z_high - z_low + 1, y_high - y_low + 1
    for zz in range(2 * z_low - 1, 2 * z_high + 2):
        for yy in range(2 * y_low - 1, 2 * y_high + 2):
            cell = tile(zz, yy)
            shifted = x_before(cell[rows - moved :].astype(f32)).astype(bf16)
            for a in range(3):
                for b in range(3):
                    i, j = zz + 1 - a, yy + 1 - b
                    if i % 2 or j % 2:
                        continue
                    i, j = i // 2 - z_low, j // 2 - y_low
                    if not (0 <= i < deep and 0 <= j < wide):
                        continue
                    top = (a * 3 + b) * step
                    out[top : top + rows, at(i * wide + j)] = cell
                    out[top + rows : top + step, at(i * wide + j)] = shifted


def finish(pre):
    square = pre * pre + 1.0
    inverse = lax.rsqrt(square)
    return 0.65 * pre + 0.35 * (square * inverse - 1.0), 0.65 + 0.35 * (pre * inverse)


def forward_body(a0, above, row, below, corner, t1, t2, t3, tt2, tt3, head, targets, inside,
                 p1, kept, slopes, sums, a1, a2):
    low = jnp.where(lane_of((32, LANES)) < HALF, 1.0, 0.0)
    upper = (1.0 - low).astype(bf16)
    upper_below = ((1.0 - low) * inside[0]).astype(bf16)
    low_row = (low * inside[1]).astype(bf16)
    low_below = (low * inside[2]).astype(bf16)
    low_corner = (low * inside[1] * inside[2]).astype(bf16)
    low = low.astype(bf16)

    def tile_one(zz, yy):
        yp = yy % 8
        part = slice(16 * (yy + 7), 16 * (yy + 8))
        if zz >= 0 and yy >= 0:
            return a0[zz, yp] * low + above[zz, yp] * upper
        if zz >= 0:
            return unpacked(row[zz, part, :]) * low_row + half_turned(above[zz, yp]) * upper
        if yy >= 0:
            got = unpacked(below[zz + 7, 16 * yp : 16 * yp + 16, :])
            return got * low_below + a0[zz + 8, yp] * upper_below
        got = unpacked(corner[zz + 7, part, :])
        return got * low_corner + half_turned(a0[zz + 8, yp]) * upper_below

    fill_patches(tile_one, (-3, 3), (-3, 3), 32, 16, p1)
    act, slopes[:, : 49 * LANES] = finish(dot(t1[...], p1[...]))
    a1[...] = act.astype(bf16)
    fill_patches(lambda z, y: a1[:, at((z + 3) * 7 + y + 3)], (-1, 1), (-1, 1), 64, 16, kept)
    act, slopes[:, AT_TWO * LANES : AT_THREE * LANES] = finish(dot(t2[...], kept[:720, : 9 * LANES]))
    a2[...] = act.astype(bf16)
    fill_patches(lambda z, y: a2[:, at((z + 1) * 3 + y + 1)], (0, 0), (0, 0), 64, 32, kept.at[:, at(9)])
    act, slopes[:, at(AT_THREE)] = finish(dot(t3[...], kept[:, at(9)]))
    column = jnp.sum(act.astype(bf16).astype(f32), axis=1, keepdims=True)
    spot = lax.broadcasted_iota(jnp.int32, (HALF, LANES), 0) == lane_of((HALF, LANES))
    line = jnp.sum(jnp.where(spot, column, 0.0), axis=0, keepdims=True)
    sums[...] = jnp.broadcast_to(line, sums.shape)
    kept[:720, at(10)] = tt2[...]
    kept[:, at(11)] = tt3[...]
    slopes[:4, AT_HEAD : AT_HEAD + HALF] = head[...]
    spot = lax.broadcasted_iota(jnp.int32, (4, 4), 0) == lane_of((4, 4))
    column = jnp.sum(jnp.where(spot, targets[...], 0.0), axis=1, keepdims=True)
    slopes[8:12, AT_HEAD : AT_HEAD + LANES] = jnp.broadcast_to(column, (4, LANES))


def reach(index):
    return [(1, index // 2)] if index % 2 == 0 else [(2, index // 2), (0, index // 2 + 1)]


def back_cell(terms, z, y, step, rows, low, high):
    total = None
    for a, i in reach(z):
        for b, j in reach(y):
            if low <= i <= high and low <= j <= high:
                top = (a * 3 + b) * step
                part = terms[top : top + step, at((i - low) * (high - low + 1) + j - low)]
                total = part if total is None else total + part
    moved = step - rows
    last = total[rows - moved : rows] + x_after(total[rows:])
    return jnp.concatenate([total[: rows - moved], last], axis=0)


def backward_body(cells, share, gathered, p1, kept, slopes,
                  result, out, err3, err2, err1, terms3, terms2):
    head = slopes[:4, AT_HEAD : AT_HEAD + HALF]
    targets = slopes[8:12, AT_HEAD : AT_HEAD + 1]
    out[...] = jnp.zeros_like(out)
    pooled = jnp.sum(gathered[...], axis=0, keepdims=True)[:, :HALF] / cells
    errors = jnp.sum(head * pooled, axis=1, keepdims=True) - targets
    outer = errors * pooled * share
    loss = 0.5 * jnp.sum(errors * errors, axis=0, keepdims=True) * share
    exact = [jnp.concatenate([outer[0:1], outer[1:2]], axis=1),
             jnp.concatenate([outer[2:3], outer[3:4]], axis=1),
             jnp.broadcast_to(loss, (1, LANES))]
    for k, value in enumerate(exact):
        first = value.astype(bf16).astype(f32)
        out[EXACT, HIGH + k : HIGH + k + 1, :] = first
        out[EXACT, LOW + k : LOW + k + 1, :] = value - first
    line = jnp.sum(errors * head, axis=0, keepdims=True) / cells
    spot = lax.broadcasted_iota(jnp.int32, (HALF, HALF), 0) == lane_of((HALF, HALF))
    back_pool = jnp.sum(jnp.where(spot, line, 0.0), axis=1, keepdims=True)

    err3[:HALF, :] = (back_pool * slopes[:, at(AT_THREE)]).astype(bf16)
    err3[HALF:, :] = jnp.zeros((HALF, LANES), bf16)
    err2[HALF:, :] = jnp.zeros((HALF, 9 * LANES), bf16)
    err1[HALF:, :] = jnp.zeros((HALF, 49 * LANES), bf16)
    terms3[...] = dot(kept[:, at(11)], err3[...])
    for k in range(9):
        back = back_cell(terms3, k // 3 - 1, k % 3 - 1, 96, 64, 0, 0)
        err2[:HALF, at(k)] = (back * slopes[:, at(AT_TWO + k)]).astype(bf16)
    terms2[...] = dot(kept[:720, at(10)], err2[...])
    for k in range(49):
        back = back_cell(terms2, k // 7 - 3, k % 7 - 3, 80, 64, -1, 1)
        err1[:HALF, at(k)] = (back * slopes[:, at(k)]).astype(bf16)

    grad = dot_nt(kept[:, at(9)], err3[...])
    taps = [96 * ab + 32 * ((e + 2) % 3) for ab in range(9) for e in range(3)]
    for k, top in enumerate(taps[:14]):
        block = grad[top : top + 32]
        if k + 14 < 27:
            other = taps[k + 14]
            block = block + pltpu.roll(grad[other : other + 32], HALF, 1)
        out[k, :32, :] = block

    grad = dot_nt(kept[:720, : 9 * LANES], err2[...])
    blocks = []
    for ab in range(9):
        x = [grad[80 * ab + 16 * i : 80 * ab + 16 * i + 16] for i in range(5)]
        for first, second in ((4, 1), (0, 2), (1, 3)):
            block = x[first] + pltpu.roll(x[second], LANES - 32, 1)
            blocks.append(jnp.where(lane_of(block.shape) < 32, block, 0.0))
    for k in range(7):
        block = blocks[k]
        for m in range(1, 4):
            if k + 7 * m < 27:
                block = block + pltpu.roll(blocks[k + 7 * m], 32 * m, 1)
        for i, (chunk, top) in enumerate(places_two(k)):
            out[chunk, top : top + 8, :] = block[8 * i : 8 * i + 8]

    grad = dot_nt(p1[...], err1[...])
    blocks = []
    for ab in range(9):
        x = [grad[48 * ab + 8 * i : 48 * ab + 8 * i + 8] for i in range(6)]
        both, low = x[0], x[5]
        for m in range(1, 4):
            both = both + pltpu.roll(x[m], LANES - 16 * m, 1)
            low = low + pltpu.roll(x[m - 1], LANES - 16 * m, 1)
        low = jnp.where(lax.broadcasted_iota(jnp.int32, low.shape, 0) >= 4, low, 0.0)
        block = jnp.concatenate([both, low], axis=0)
        blocks.append(jnp.where(lane_of(block.shape) < 16, block, 0.0))
    block = blocks[0]
    for m in range(1, 8):
        block = block + pltpu.roll(blocks[m], 16 * m, 1)
    for m, block in enumerate((block, blocks[8])):
        for i, (chunk, top) in enumerate(places_one(m)):
            out[chunk, top : top + 8, :] = block[8 * i : 8 * i + 8]
    result[...] = out[...].astype(bf16)


def places_two(k):
    if k < 4:
        return [(14 + k // 2, 16 * (k % 2)), (14 + k // 2, 16 * (k % 2) + 8)]
    return [(2 * k - 8, 32), (2 * k - 7, 32)]


def places_one(m):
    return [(6 + 2 * m, 32), (7 + 2 * m, 32)]


def total_body(parts, chunk, out):
    total = parts[0].astype(f32)
    for k in range(1, parts.shape[0]):
        total = total + parts[k].astype(f32)
    exact = total[HIGH:LOW] + total[LOW : LOW + 3]
    first = exact.astype(bf16).astype(f32)
    tail = jnp.concatenate([first, exact - first, total[LOW + 3 :]], axis=0)
    tail = jnp.where(chunk[0] == EXACT, tail, total[HIGH:])
    total = jnp.concatenate([total[:HIGH], tail], axis=0).astype(bf16)
    for k in range(out.shape[0]):
        out[k] = total


def update_body(sent, u1, u2, u3, uh, loss, total):
    total[...] = sent[...].astype(f32)

    def scale(blocks, count):
        mean = 0.0
        for block in blocks:
            squares = jnp.sum(block * block, axis=0, keepdims=True)
            mean = mean + jnp.sum(squares, axis=1, keepdims=True) / count
        return 1.0 / jnp.sqrt(mean + epsilon)

    def read(places):
        return jnp.concatenate([total[chunk, top : top + 8, :] for chunk, top in places], axis=0)

    blocks = [total[k, :32, :] for k in range(14)]
    factor = scale(blocks, 64 * 32 * 27)
    for k, block in enumerate(blocks):
        block = block * factor
        u3[k] = block[:, :HALF]
        if k + 14 < 27:
            u3[k + 14] = pltpu.roll(block, HALF, 1)[:, :HALF]
    blocks = [read(places_two(k)) for k in range(7)]
    factor = scale(blocks, 32 * 16 * 27)
    for k, block in enumerate(blocks):
        block = block * factor
        for m in range(4):
            if k + 7 * m < 27:
                u2[k + 7 * m] = (pltpu.roll(block, LANES - 32 * m, 1) if m else block)[:, :32]
    blocks = [read(places_one(m)) for m in range(2)]
    factor = scale(blocks, 16 * 4 * 27)
    for ab in range(9):
        m = ab % 8
        block = blocks[ab // 8] * factor
        block = (pltpu.roll(block, LANES - 16 * m, 1) if m else block)[:, :16]
        u1[3 * ab] = block[12:16]
        u1[3 * ab + 1] = block[0:4]
        u1[3 * ab + 2] = block[4:8]
    exact = [total[EXACT, HIGH + k : HIGH + k + 1, :] + total[EXACT, LOW + k : LOW + k + 1, :]
             for k in range(3)]
    factor = scale(exact[:2], 4 * 64)
    for k in range(2):
        line = exact[k] * factor
        uh[2 * k : 2 * k + 1, :] = line[:, :HALF]
        uh[2 * k + 1 : 2 * k + 2, :] = pltpu.roll(line, HALF, 1)[:, :HALF]
    loss[...] = exact[2]


def exchange(whole, row, below, corner):
    gz, gy = lax.axis_size("gz"), lax.axis_size("gy")
    z, y = [(i, (i + 1) % gz) for i in range(gz)], [(i, (i + 1) % gy) for i in range(gy)]
    both = [(i * gy + j, k * gy + l) for i, k in z for j, l in y]
    above = lax.ppermute(whole, "gz", [(k, i) for i, k in z])
    below = lax.ppermute(below, "gz", z)
    corner = lax.ppermute(corner, ("gz", "gy"), both)
    return above, lax.ppermute(row, "gy", y), below, corner


def summed_over_all(parts, chunk):
    beyond = lax.axis_size(("batch", "gz"))
    spaces = (pltpu.VMEM, pltpu.SMEM)
    parts = lax.all_to_all(parts, "gy", 0, 0, tiled=True)
    (parts,) = call(total_body, [((beyond, ROWS, LANES), bf16)], (parts, chunk), spaces=spaces)
    parts = lax.all_to_all(parts, ("batch", "gz"), 0, 0, tiled=True)
    (parts,) = call(total_body, [((CHUNKS, ROWS, LANES), bf16)], (parts, chunk), spaces=spaces)
    return lax.all_to_all(parts, "gy", 0, 0, tiled=True)


def local(volume, conv_one, conv_two, conv_three, head_weight, targets):
    devices = lax.axis_size("gz") * lax.axis_size("gy")
    cells = float(devices * LANES)
    z_at, y_at = lax.axis_index("gz"), lax.axis_index("gy")
    inside = jnp.stack([z_at < lax.axis_size("gz") - 1, y_at > 0, z_at > 0]).astype(f32)
    chunk = y_at.astype(jnp.int32).reshape(1)
    volume, chunk, inside = lax.optimization_barrier((volume, chunk, inside))

    def taps(w):
        w = jnp.transpose(w, (2, 3, 4, 1, 0)).astype(f32)
        return jnp.pad(w.reshape((27,) + w.shape[3:]), ((0, 0), (0, 0), (0, LANES - w.shape[4])))

    w1 = taps(conv_one).reshape(9, 3, 4, LANES)
    both = w1[:, 1:].reshape(9, 1, 8, LANES)
    low = jnp.pad(w1[:, :1], ((0, 0), (0, 0), (4, 0), (0, 0)))
    t1, t2, t3, tt2, tt3 = call(
        weights_body,
        [((64, 432), bf16), ((64, 720), bf16), ((64, 864), bf16), ((720, LANES), bf16), ((864, LANES), bf16)],
        (jnp.concatenate([both, low], axis=1), taps(conv_two), taps(conv_three)),
    )
    a0, row, below, corner = call(
        arrange_body,
        [((8, 8, 32, LANES), bf16), ((8, 112, LANES), bf16), ((7, LANES, LANES), bf16), ((7, 112, LANES), bf16)],
        (volume.reshape(512, 512),),
        [((512, 512), f32)],
    )
    above, row, below, corner = exchange(a0, row, below, corner)
    p1, kept, slopes, sums = call(
        forward_body,
        [((432, 49 * LANES), bf16), ((864, 12 * LANES), bf16), ((64, 60 * LANES), f32), ((devices, LANES), f32)],
        (a0, above, row, below, corner, t1, t2, t3, tt2, tt3, head_weight, targets, inside),
        [((64, 49 * LANES), bf16), ((64, 9 * LANES), bf16)],
        24,
        [pltpu.VMEM] * 12 + [pltpu.SMEM],
    )
    pooled = lax.all_to_all(sums, ("gz", "gy"), 0, 0, tiled=True)
    (flat,) = call(
        functools.partial(backward_body, cells, 1.0 / devices),
        [((CHUNKS, ROWS, LANES), bf16)],
        (pooled, p1, kept, slopes),
        [((CHUNKS, ROWS, LANES), f32), ((LANES, LANES), bf16), ((LANES, 9 * LANES), bf16),
         ((LANES, 49 * LANES), bf16), ((864, LANES), f32), ((720, 9 * LANES), f32)],
        24,
    )
    u1, u2, u3, uh, loss = call(
        update_body,
        [((27, 4, 16), f32), ((27, 16, 32), f32), ((27, 32, 64), f32), ((4, 64), f32), ((1, LANES), f32)],
        (summed_over_all(flat, chunk),),
        [((CHUNKS, ROWS, LANES), f32)],
    )

    def kernel_form(u):
        return jnp.transpose(u.reshape((3, 3, 3) + u.shape[1:]), (4, 3, 0, 1, 2))

    return kernel_form(u1), kernel_form(u2), kernel_form(u3), uh, loss[0, 0]


def solution(mesh):
    in_specs = (P("batch", None, "gz", "gy", None), P(), P(), P(), P(), P("batch", None))
    out_specs = (P(), P(), P(), P(), P())
    return jax.shard_map(local, mesh=mesh, in_specs=in_specs, out_specs=out_specs, check_vma=False)
```

```python
import functools
import jax
import jax.numpy as jnp
from jax import lax
from jax.experimental import pallas as pl
from jax.experimental.pallas import tpu as pltpu
from jax.sharding import PartitionSpec as P

epsilon = 1e-06
f32 = jnp.float32
bf16 = jnp.bfloat16
LANES = 128
HALF = 64
CHUNKS, ROWS = 16, 40
EXACT, HIGH, LOW = 10, 32, 35
AT_TWO, AT_THREE, AT_HEAD = 49, 58, 59 * LANES


def call(body, outs, args, scratch=(), mib=8, spaces=None):
    return pl.pallas_call(
        body,
        out_shape=[jax.ShapeDtypeStruct(s, d) for s, d in outs],
        in_specs=[pl.BlockSpec(memory_space=m) for m in spaces or [pltpu.VMEM] * len(args)],
        out_specs=[pl.BlockSpec(memory_space=pltpu.VMEM)] * len(outs),
        scratch_shapes=[pltpu.VMEM(*s) if isinstance(s, tuple) else s for s in scratch],
        compiler_params=pltpu.CompilerParams(vmem_limit_bytes=mib * 1024 * 1024),
    )(*args)


def lane_of(shape):
    return lax.broadcasted_iota(jnp.int32, shape, len(shape) - 1)


def dot(a, b):
    return lax.dot_general(a, b, (((1,), (0,)), ((), ())), preferred_element_type=f32)


def dot_nt(a, b):
    return lax.dot_general(a, b, (((1,), (1,)), ((), ())), preferred_element_type=f32)


def upper_half(tile):
    top, bottom = tile[:16].astype(f32), tile[16:].astype(f32)
    return jnp.where(lane_of(top.shape) < HALF, pltpu.roll(top, HALF, 1), bottom).astype(bf16)


def lower_half(tile):
    top, bottom = tile[:16].astype(f32), tile[16:].astype(f32)
    return jnp.where(lane_of(top.shape) < HALF, top, pltpu.roll(bottom, HALF, 1)).astype(bf16)


def unpacked(received):
    turned = pltpu.roll(received.astype(f32), HALF, 1).astype(bf16)
    return jnp.concatenate([received, turned], axis=0)


def half_turned(tile):
    return pltpu.roll(tile.astype(f32), HALF, 1).astype(bf16)


def x_before(rows):
    return jnp.where(lane_of(rows.shape) % HALF == 0, 0.0, pltpu.roll(rows, 1, 1))


def x_after(rows):
    return jnp.where(lane_of(rows.shape) % HALF == HALF - 1, 0.0, pltpu.roll(rows, LANES - 1, 1))


def at(group):
    return slice(group * LANES, (group + 1) * LANES)


def arrange_body(vol, a0, up, row, below, corner, rows):
    for z in range(8):
        tops = [c * 128 + z * 16 + yb * 8 for yb in range(2) for c in range(4)]
        cube = jnp.stack([vol[top : top + 8, :] for top in tops], axis=0)
        rows[z * 64 : z * 64 + 64, :] = jnp.transpose(cube, (1, 0, 2)).reshape(64, 512)
    x_at = lax.broadcasted_iota(jnp.int32, (512, 512), 0)
    to = lax.broadcasted_iota(jnp.int32, (512, 512), 1)
    move = jnp.where(x_at == (to % HALF) * 8 + to // HALF, 1.0, 0.0).astype(bf16)
    phased = dot(rows[...].astype(bf16), move)
    parts = []
    for j in range(4):
        part = phased[:, at(j)].reshape(64, 8, LANES)
        turned = pltpu.roll(pltpu.roll(part, 4, 1), HALF, 2)
        sub = lax.broadcasted_iota(jnp.int32, part.shape, 1)
        parts.append(jnp.where((sub < 4) == (lane_of(part.shape) < HALF), part, turned))
    whole = jnp.concatenate(parts, axis=1).astype(bf16)
    a0[...] = whole.reshape(8, 8, 32, LANES)
    for z in range(8):
        up[z, :16, :] = upper_half(a0[z, 0])
        for yp in range(8):
            if yp > 0:
                up[z, 32 * yp - 16 : 32 * yp + 16, :] = a0[z, yp]
            if z > 0:
                below[z - 1, 16 * yp : 16 * yp + 16, :] = lower_half(a0[z, yp])
        for yp in range(1, 8):
            half = upper_half(a0[z, yp])
            row[z, 16 * yp - 16 : 16 * yp, :] = half
            if z > 0:
                corner[z - 1, 16 * yp - 16 : 16 * yp, :] = half


def weights_body(w1, w2, w3, t1, t2, t3, tt2, tt3):
    eye = jnp.where(
        lax.broadcasted_iota(jnp.int32, (HALF, LANES), 0) == lane_of((HALF, LANES)), 1.0, 0.0
    ).astype(bf16)
    blocks = []
    for ab in range(9):
        both, low = w1[ab, 0], w1[ab, 1]
        for m in range(4):
            block = pltpu.roll(both, 16 * m, 1) if m else both
            if m < 3:
                block = block + pltpu.roll(low, 16 * (m + 1), 1)
            blocks.append(block)
        blocks += [jnp.zeros_like(low), low]
    t1[...] = dot_nt(eye, jnp.concatenate(blocks, axis=0).astype(bf16)).astype(bf16)
    blocks = []
    for ab in range(9):
        e0, e1, e2 = w2[3 * ab], w2[3 * ab + 1], w2[3 * ab + 2]
        blocks += [e1, e2 + pltpu.roll(e0, 32, 1), pltpu.roll(e1, 32, 1), pltpu.roll(e2, 32, 1), e0]
    tt2[...] = jnp.concatenate(blocks, axis=0).astype(bf16)
    t2[...] = dot_nt(eye, tt2[...]).astype(bf16)
    blocks = []
    for ab in range(9):
        blocks += [w3[3 * ab + 1], w3[3 * ab + 2], w3[3 * ab]]
    tt3[...] = jnp.concatenate(blocks, axis=0).astype(bf16)
    t3[...] = dot_nt(eye, tt3[...]).astype(bf16)


def fill_patches(tile, z_range, y_range, rows, moved, out):
    (z_low, z_high), (y_low, y_high) = z_range, y_range
    step, deep, wide = rows + moved, z_high - z_low + 1, y_high - y_low + 1
    for zz in range(2 * z_low - 1, 2 * z_high + 2):
        for yy in range(2 * y_low - 1, 2 * y_high + 2):
            cell = tile(zz, yy)
            shifted = x_before(cell[rows - moved :].astype(f32)).astype(bf16)
            for a in range(3):
                for b in range(3):
                    i, j = zz + 1 - a, yy + 1 - b
                    if i % 2 or j % 2:
                        continue
                    i, j = i // 2 - z_low, j // 2 - y_low
                    if not (0 <= i < deep and 0 <= j < wide):
                        continue
                    top = (a * 3 + b) * step
                    out[top : top + rows, at(i * wide + j)] = cell
                    out[top + rows : top + step, at(i * wide + j)] = shifted


def finish(pre):
    square = pre * pre + 1.0
    inverse = lax.rsqrt(square)
    return 0.65 * pre + 0.35 * (square * inverse - 1.0), 0.65 + 0.35 * (pre * inverse)


def forward_body(a0, above, row, below, corner, t1, t2, t3, tt2, tt3, head, targets, inside,
                 p1, kept, slopes, sums, a1, a2):
    low = jnp.where(lane_of((32, LANES)) < HALF, 1.0, 0.0)
    upper = (1.0 - low).astype(bf16)
    upper_below = ((1.0 - low) * inside[0]).astype(bf16)
    low_row = (low * inside[1]).astype(bf16)
    low_below = (low * inside[2]).astype(bf16)
    low_corner = (low * inside[1] * inside[2]).astype(bf16)
    low = low.astype(bf16)

    def tile_one(zz, yy):
        yp = yy % 8
        part = slice(16 * (yy + 7), 16 * (yy + 8))
        if zz >= 0 and yy >= 0:
            if yp > 0:
                return a0[zz, yp] * low + above[zz, 32 * yp - 16 : 32 * yp + 16, :] * upper
            got = above[zz, :16, :]
            return a0[zz, yp] * low + jnp.concatenate([half_turned(got), got], axis=0) * upper
        if zz >= 0:
            return unpacked(row[zz, part, :]) * low_row + half_turned(above[zz, 32 * yp - 16 : 32 * yp + 16, :]) * upper
        if yy >= 0:
            got = unpacked(below[zz + 7, 16 * yp : 16 * yp + 16, :])
            return got * low_below + a0[zz + 8, yp] * upper_below
        got = unpacked(corner[zz + 7, part, :])
        return got * low_corner + half_turned(a0[zz + 8, yp]) * upper_below

    fill_patches(tile_one, (-3, 3), (-3, 3), 32, 16, p1)
    act, slopes[:, : 49 * LANES] = finish(dot(t1[...], p1[...]))
    a1[...] = act.astype(bf16)
    fill_patches(lambda z, y: a1[:, at((z + 3) * 7 + y + 3)], (-1, 1), (-1, 1), 64, 16, kept)
    act, slopes[:, AT_TWO * LANES : AT_THREE * LANES] = finish(dot(t2[...], kept[:720, : 9 * LANES]))
    a2[...] = act.astype(bf16)
    fill_patches(lambda z, y: a2[:, at((z + 1) * 3 + y + 1)], (0, 0), (0, 0), 64, 32, kept.at[:, at(9)])
    act, slopes[:, at(AT_THREE)] = finish(dot(t3[...], kept[:, at(9)]))
    column = jnp.sum(act.astype(bf16).astype(f32), axis=1, keepdims=True)
    spot = lax.broadcasted_iota(jnp.int32, (HALF, LANES), 0) == lane_of((HALF, LANES))
    line = jnp.sum(jnp.where(spot, column, 0.0), axis=0, keepdims=True)
    sums[...] = jnp.broadcast_to(line, sums.shape)
    kept[:720, at(10)] = tt2[...]
    kept[:, at(11)] = tt3[...]
    slopes[:4, AT_HEAD : AT_HEAD + HALF] = head[...]
    spot = lax.broadcasted_iota(jnp.int32, (4, 4), 0) == lane_of((4, 4))
    column = jnp.sum(jnp.where(spot, targets[...], 0.0), axis=1, keepdims=True)
    slopes[8:12, AT_HEAD : AT_HEAD + LANES] = jnp.broadcast_to(column, (4, LANES))


def reach(index):
    return [(1, index // 2)] if index % 2 == 0 else [(2, index // 2), (0, index // 2 + 1)]


def back_cell(terms, z, y, step, rows, low, high):
    total = None
    for a, i in reach(z):
        for b, j in reach(y):
            if low <= i <= high and low <= j <= high:
                top = (a * 3 + b) * step
                part = terms[top : top + step, at((i - low) * (high - low + 1) + j - low)]
                total = part if total is None else total + part
    moved = step - rows
    last = total[rows - moved : rows] + x_after(total[rows:])
    return jnp.concatenate([total[: rows - moved], last], axis=0)


def backward_body(cells, share, gathered, p1, kept, slopes,
                  result, out, err3, err2, err1, terms3, terms2):
    head = slopes[:4, AT_HEAD : AT_HEAD + HALF]
    targets = slopes[8:12, AT_HEAD : AT_HEAD + 1]
    out[...] = jnp.zeros_like(out)
    pooled = jnp.sum(gathered[...], axis=0, keepdims=True)[:, :HALF] / cells
    errors = jnp.sum(head * pooled, axis=1, keepdims=True) - targets
    outer = errors * pooled * share
    loss = 0.5 * jnp.sum(errors * errors, axis=0, keepdims=True) * share
    exact = [jnp.concatenate([outer[0:1], outer[1:2]], axis=1),
             jnp.concatenate([outer[2:3], outer[3:4]], axis=1),
             jnp.broadcast_to(loss, (1, LANES))]
    for k, value in enumerate(exact):
        first = value.astype(bf16).astype(f32)
        out[EXACT, HIGH + k : HIGH + k + 1, :] = first
        out[EXACT, LOW + k : LOW + k + 1, :] = value - first
    line = jnp.sum(errors * head, axis=0, keepdims=True) / cells
    spot = lax.broadcasted_iota(jnp.int32, (HALF, HALF), 0) == lane_of((HALF, HALF))
    back_pool = jnp.sum(jnp.where(spot, line, 0.0), axis=1, keepdims=True)

    err3[:HALF, :] = (back_pool * slopes[:, at(AT_THREE)]).astype(bf16)
    err3[HALF:, :] = jnp.zeros((HALF, LANES), bf16)
    err2[HALF:, :] = jnp.zeros((HALF, 9 * LANES), bf16)
    err1[HALF:, :] = jnp.zeros((HALF, 49 * LANES), bf16)
    terms3[...] = dot(kept[:, at(11)], err3[...])
    for k in range(9):
        back = back_cell(terms3, k // 3 - 1, k % 3 - 1, 96, 64, 0, 0)
        err2[:HALF, at(k)] = (back * slopes[:, at(AT_TWO + k)]).astype(bf16)
    terms2[...] = dot(kept[:720, at(10)], err2[...])
    for k in range(49):
        back = back_cell(terms2, k // 7 - 3, k % 7 - 3, 80, 64, -1, 1)
        err1[:HALF, at(k)] = (back * slopes[:, at(k)]).astype(bf16)

    grad = dot_nt(kept[:, at(9)], err3[...])
    taps = [96 * ab + 32 * ((e + 2) % 3) for ab in range(9) for e in range(3)]
    for k, top in enumerate(taps[:14]):
        block = grad[top : top + 32]
        if k + 14 < 27:
            other = taps[k + 14]
            block = block + pltpu.roll(grad[other : other + 32], HALF, 1)
        out[k, :32, :] = block

    grad = dot_nt(kept[:720, : 9 * LANES], err2[...])
    blocks = []
    for ab in range(9):
        x = [grad[80 * ab + 16 * i : 80 * ab + 16 * i + 16] for i in range(5)]
        for first, second in ((4, 1), (0, 2), (1, 3)):
            block = x[first] + pltpu.roll(x[second], LANES - 32, 1)
            blocks.append(jnp.where(lane_of(block.shape) < 32, block, 0.0))
    for k in range(7):
        block = blocks[k]
        for m in range(1, 4):
            if k + 7 * m < 27:
                block = block + pltpu.roll(blocks[k + 7 * m], 32 * m, 1)
        for i, (chunk, top) in enumerate(places_two(k)):
            out[chunk, top : top + 8, :] = block[8 * i : 8 * i + 8]

    grad = dot_nt(p1[...], err1[...])
    blocks = []
    for ab in range(9):
        x = [grad[48 * ab + 8 * i : 48 * ab + 8 * i + 8] for i in range(6)]
        both, low = x[0], x[5]
        for m in range(1, 4):
            both = both + pltpu.roll(x[m], LANES - 16 * m, 1)
            low = low + pltpu.roll(x[m - 1], LANES - 16 * m, 1)
        low = jnp.where(lax.broadcasted_iota(jnp.int32, low.shape, 0) >= 4, low, 0.0)
        block = jnp.concatenate([both, low], axis=0)
        blocks.append(jnp.where(lane_of(block.shape) < 16, block, 0.0))
    block = blocks[0]
    for m in range(1, 8):
        block = block + pltpu.roll(blocks[m], 16 * m, 1)
    for m, block in enumerate((block, blocks[8])):
        for i, (chunk, top) in enumerate(places_one(m)):
            out[chunk, top : top + 8, :] = block[8 * i : 8 * i + 8]
    result[...] = out[...].astype(bf16)


def places_two(k):
    if k < 4:
        return [(14 + k // 2, 16 * (k % 2)), (14 + k // 2, 16 * (k % 2) + 8)]
    return [(2 * k - 8, 32), (2 * k - 7, 32)]


def places_one(m):
    return [(6 + 2 * m, 32), (7 + 2 * m, 32)]


def total_body(parts, chunk, out):
    total = parts[0].astype(f32)
    for k in range(1, parts.shape[0]):
        total = total + parts[k].astype(f32)
    exact = total[HIGH:LOW] + total[LOW : LOW + 3]
    first = exact.astype(bf16).astype(f32)
    tail = jnp.concatenate([first, exact - first, total[LOW + 3 :]], axis=0)
    tail = jnp.where(chunk[0] == EXACT, tail, total[HIGH:])
    total = jnp.concatenate([total[:HIGH], tail], axis=0).astype(bf16)
    for k in range(out.shape[0]):
        out[k] = total


def update_body(sent, u1, u2, u3, uh, loss, total):
    total[...] = sent[...].astype(f32)

    def scale(blocks, count):
        mean = 0.0
        for block in blocks:
            squares = jnp.sum(block * block, axis=0, keepdims=True)
            mean = mean + jnp.sum(squares, axis=1, keepdims=True) / count
        return 1.0 / jnp.sqrt(mean + epsilon)

    def read(places):
        return jnp.concatenate([total[chunk, top : top + 8, :] for chunk, top in places], axis=0)

    blocks = [total[k, :32, :] for k in range(14)]
    factor = scale(blocks, 64 * 32 * 27)
    for k, block in enumerate(blocks):
        block = block * factor
        u3[k] = block[:, :HALF]
        if k + 14 < 27:
            u3[k + 14] = pltpu.roll(block, HALF, 1)[:, :HALF]
    blocks = [read(places_two(k)) for k in range(7)]
    factor = scale(blocks, 32 * 16 * 27)
    for k, block in enumerate(blocks):
        block = block * factor
        for m in range(4):
            if k + 7 * m < 27:
                u2[k + 7 * m] = (pltpu.roll(block, LANES - 32 * m, 1) if m else block)[:, :32]
    blocks = [read(places_one(m)) for m in range(2)]
    factor = scale(blocks, 16 * 4 * 27)
    for ab in range(9):
        m = ab % 8
        block = blocks[ab // 8] * factor
        block = (pltpu.roll(block, LANES - 16 * m, 1) if m else block)[:, :16]
        u1[3 * ab] = block[12:16]
        u1[3 * ab + 1] = block[0:4]
        u1[3 * ab + 2] = block[4:8]
    exact = [total[EXACT, HIGH + k : HIGH + k + 1, :] + total[EXACT, LOW + k : LOW + k + 1, :]
             for k in range(3)]
    factor = scale(exact[:2], 4 * 64)
    for k in range(2):
        line = exact[k] * factor
        uh[2 * k : 2 * k + 1, :] = line[:, :HALF]
        uh[2 * k + 1 : 2 * k + 2, :] = pltpu.roll(line, HALF, 1)[:, :HALF]
    loss[...] = exact[2]


def exchange(whole, row, below, corner):
    gz, gy = lax.axis_size("gz"), lax.axis_size("gy")
    z, y = [(i, (i + 1) % gz) for i in range(gz)], [(i, (i + 1) % gy) for i in range(gy)]
    both = [(i * gy + j, k * gy + l) for i, k in z for j, l in y]
    above = lax.ppermute(whole, "gz", [(k, i) for i, k in z])
    below = lax.ppermute(below, "gz", z)
    corner = lax.ppermute(corner, ("gz", "gy"), both)
    return above, lax.ppermute(row, "gy", y), below, corner


def summed_over_all(parts, chunk):
    beyond = lax.axis_size(("batch", "gz"))
    spaces = (pltpu.VMEM, pltpu.SMEM)
    parts = lax.all_to_all(parts, "gy", 0, 0, tiled=True)
    (parts,) = call(total_body, [((beyond, ROWS, LANES), bf16)], (parts, chunk), spaces=spaces)
    parts = lax.all_to_all(parts, ("batch", "gz"), 0, 0, tiled=True)
    (parts,) = call(total_body, [((CHUNKS, ROWS, LANES), bf16)], (parts, chunk), spaces=spaces)
    return lax.all_to_all(parts, "gy", 0, 0, tiled=True)


def local(volume, conv_one, conv_two, conv_three, head_weight, targets):
    devices = lax.axis_size("gz") * lax.axis_size("gy")
    cells = float(devices * LANES)
    z_at, y_at = lax.axis_index("gz"), lax.axis_index("gy")
    inside = jnp.stack([z_at < lax.axis_size("gz") - 1, y_at > 0, z_at > 0]).astype(f32)
    chunk = y_at.astype(jnp.int32).reshape(1)
    volume, chunk, inside = lax.optimization_barrier((volume, chunk, inside))

    def taps(w):
        w = jnp.transpose(w, (2, 3, 4, 1, 0)).astype(f32)
        return jnp.pad(w.reshape((27,) + w.shape[3:]), ((0, 0), (0, 0), (0, LANES - w.shape[4])))

    w1 = taps(conv_one).reshape(9, 3, 4, LANES)
    both = w1[:, 1:].reshape(9, 1, 8, LANES)
    low = jnp.pad(w1[:, :1], ((0, 0), (0, 0), (4, 0), (0, 0)))
    t1, t2, t3, tt2, tt3 = call(
        weights_body,
        [((64, 432), bf16), ((64, 720), bf16), ((64, 864), bf16), ((720, LANES), bf16), ((864, LANES), bf16)],
        (jnp.concatenate([both, low], axis=1), taps(conv_two), taps(conv_three)),
    )
    a0, up, row, below, corner = call(
        arrange_body,
        [((8, 8, 32, LANES), bf16), ((8, 240, LANES), bf16), ((8, 112, LANES), bf16), ((7, LANES, LANES), bf16), ((7, 112, LANES), bf16)],
        (volume.reshape(512, 512),),
        [((512, 512), f32)],
    )
    above, row, below, corner = exchange(up, row, below, corner)
    p1, kept, slopes, sums = call(
        forward_body,
        [((432, 49 * LANES), bf16), ((864, 12 * LANES), bf16), ((64, 60 * LANES), f32), ((devices, LANES), f32)],
        (a0, above, row, below, corner, t1, t2, t3, tt2, tt3, head_weight, targets, inside),
        [((64, 49 * LANES), bf16), ((64, 9 * LANES), bf16)],
        24,
        [pltpu.VMEM] * 12 + [pltpu.SMEM],
    )
    pooled = lax.all_to_all(sums, ("gz", "gy"), 0, 0, tiled=True)
    (flat,) = call(
        functools.partial(backward_body, cells, 1.0 / devices),
        [((CHUNKS, ROWS, LANES), bf16)],
        (pooled, p1, kept, slopes),
        [((CHUNKS, ROWS, LANES), f32), ((LANES, LANES), bf16), ((LANES, 9 * LANES), bf16),
         ((LANES, 49 * LANES), bf16), ((864, LANES), f32), ((720, 9 * LANES), f32)],
        24,
    )
    u1, u2, u3, uh, loss = call(
        update_body,
        [((27, 4, 16), f32), ((27, 16, 32), f32), ((27, 32, 64), f32), ((4, 64), f32), ((1, LANES), f32)],
        (summed_over_all(flat, chunk),),
        [((CHUNKS, ROWS, LANES), f32)],
    )

    def kernel_form(u):
        return jnp.transpose(u.reshape((3, 3, 3) + u.shape[1:]), (4, 3, 0, 1, 2))

    return kernel_form(u1), kernel_form(u2), kernel_form(u3), uh, loss[0, 0]


def solution(mesh):
    in_specs = (P("batch", None, "gz", "gy", None), P(), P(), P(), P(), P("batch", None))
    out_specs = (P(), P(), P(), P(), P())
    return jax.shard_map(local, mesh=mesh, in_specs=in_specs, out_specs=out_specs, check_vma=False)
```
